32 devices in a mesh: wide: 16 (over z, y, core), narrow: 2 (over x).
Axes of the slice: x: 2, y: 2, z: 4, core: 2. Of those that a mesh axis runs over, the one named last changes fastest.
Arguments:
- train_points: float32 [512, 3, 256], P('wide'), may hold values from 0 to 2
- train_weights: bfloat16 [512, 256, 128], P(('wide', 'narrow')), may hold values from -1 to 1
- train_counts: int32 [512], P('wide'), may hold values from 64 to 256
- test_points: float32 [64, 3, 128], P(('wide', 'narrow')), may hold values from 0 to 2
- prior: bfloat16 [64, 128, 128], P(('wide', 'narrow')), may hold values from -6 to 6
- test_counts: int32 [64], P(('wide', 'narrow')), may hold values from 32 to 128
- pair_count: int32 [512], P('wide'), may hold values from 1 to 40, as said below
- pair_slot: int32 [16, 1280], P('wide'), may hold values from 0 to 15
- slot_tile: int32 [16, 16], replicated, may hold values from 0 to 3
Outputs:
- posterior: bfloat16 [64, 128, 128], P(('wide', 'narrow'))
The draws below stay inside these ranges and needn't reach their ends.
Inputs may be any that keep to these rules, and one draw needn't show every extreme that they name: `pair_count`: each training tile has 1 to 40 pairs; in every draw all 16 tiles of some one device have 40. `pair_slot`: positions of a group's list at or past the sum of its tiles' pair counts are not read.
All inputs are finite; a program needn't handle non-finite values.
Results may differ from the reference program's by a relative error of at most 0.0041.
Values may be sent and summed in bfloat16 or wider, within the bound.
No kernel may reach another device: no remote copies, remote signals or barrier semaphores. Data moves between devices by JAX's collectives and lax.ppermute only.
A program may use at most 64 MiB of HBM per device.

```python
import jax
import jax.numpy as jnp
from jax import lax

TILE = 256
TT = 128
S = 128
TR_DEV = 16
TE_DEV = 2
CMAX = 40
TE_GRP = 4
NTR = 512
NTE = 64
GP = 1280
N_WIDE = 16
N_NARROW = 2


def draw_pair_count(key, part):
    count_key, full_key = jax.random.split(key)
    counts = jax.random.randint(count_key, (NTR,), 1, CMAX + 1)
    full_block = jax.random.randint(full_key, (), 0, NTR // TR_DEV)
    block_ids = jnp.arange(NTR, dtype=jnp.int32) // TR_DEV
    return jnp.where(block_ids == full_block, CMAX, counts).astype(jnp.int32)


def plant(result, stream_key, smallest, high):
    longest = result.shape.index(max(result.shape))
    spots = []
    for shift in (0, 1):
        where = [jax.random.randint(jax.random.fold_in(stream_key, axis), (), 0, length) for axis, length in enumerate(result.shape)]
        where[longest] = (where[longest] + shift) % result.shape[longest]
        spots.append(tuple(where))
    return result.at[spots[0]].set(smallest).at[spots[1]].set(high)


def block_scale(rng, extent, cuts, least, largest):
    gain, own = 1.0, jax.random.fold_in(rng, 6)
    for dim, parts in cuts:
        heights = jnp.exp(jax.random.uniform(jax.random.fold_in(own, dim), (parts,), jnp.float32, least / len(cuts), largest / len(cuts)))
        gain = gain * jnp.repeat(heights, extent[dim] // parts).reshape([-1 if axis == dim else 1 for axis in range(len(extent))])
    return gain


def centred(own_key, shape, scale, reach, cuts=(), held_as=jnp.bfloat16):
    drawn = scale * jax.random.normal(own_key, shape, jnp.float32)
    if cuts:
        drawn = drawn * block_scale(own_key, shape, cuts, -0.22, 0.18)
    return jnp.clip(drawn, -reach, reach).astype(held_as)


def setup_inputs(seed: int = 0) -> dict:
    key_of = jax.random.split(jax.random.key(seed), 10)
    train_points = jnp.clip(2.0 * jax.random.uniform(key_of[0], (NTR, 3, TILE), jnp.float32) ** block_scale(key_of[0], (NTR, 3, TILE), ((0, 16),), -0.2, 0.2), 0.0, 2.0)
    train_weights = centred(key_of[1], (NTR, TILE, S), (20.0 / (TR_DEV * (CMAX + 1) * TILE / TE_DEV) ** 0.5), 1.0, ((0, 32),))
    train_counts = plant(jax.random.randint(key_of[2], (NTR,), TILE // 4, TILE + 1), jax.random.fold_in(key_of[2], 1), TILE // 4, TILE).astype(jnp.int32)
    test_points = jnp.clip(2.0 * jax.random.uniform(key_of[3], (NTE, 3, TT), jnp.float32) ** block_scale(key_of[3], (NTE, 3, TT), ((0, 32),), -0.2, 0.2), 0.0, 2.0)
    prior = centred(key_of[4], (NTE, TT, S), 1.0, 6.0, ((0, 32),))
    test_counts = plant(jax.random.randint(key_of[5], (NTE,), TT // 4, TT + 1), jax.random.fold_in(key_of[5], 1), TT // 4, TT).astype(jnp.int32)
    pair_count = draw_pair_count(jax.random.fold_in(key_of[9], 71), 0)
    pair_slot = plant(jax.random.randint(key_of[7], (N_WIDE, GP), 0, N_WIDE), jax.random.fold_in(key_of[7], 1), 0, N_WIDE - 1).astype(jnp.int32)
    slot_tile = plant(jax.random.randint(key_of[8], (N_WIDE, N_WIDE), 0, TE_GRP), jax.random.fold_in(key_of[8], 1), 0, TE_GRP - 1).astype(jnp.int32)
    return {"train_points": train_points, "train_weights": train_weights, "train_counts": train_counts, "test_points": test_points, "prior": prior, "test_counts": test_counts, "pair_count": pair_count, "pair_slot": pair_slot, "slot_tile": slot_tile}


radius = 1.0
reference_block = 32

def wendland(test_rows, train_rows):
    spread = test_rows[:, 0, :, None] - train_rows[:, 0, None, :]
    square = spread * spread
    for coord_id in (1, 2):
        spread = test_rows[:, coord_id, :, None] - train_rows[:, coord_id, None, :]
        square = square + spread * spread
    scaled = jnp.sqrt(square) / radius
    falloff = jnp.maximum(1.0 - scaled, 0.0)
    return falloff ** 4 * (4.0 * scaled + 1.0)

def reference(train_points, train_weights, train_counts, test_points, prior, test_counts, pair_count, pair_slot, slot_tile):
    train_group = TR_DEV * N_NARROW
    test_group = TE_DEV * N_NARROW
    list_length = train_group * CMAX
    lane_ids = jnp.arange(TILE, dtype=jnp.int32)
    masked = jnp.where((lane_ids[None, :] < train_counts[:, None])[:, :, None], train_weights, jnp.zeros((), train_weights.dtype))
    offsets = jnp.arange(reference_block, dtype=jnp.int32)

    def group_step(accumulated, group_id):
        counts = lax.dynamic_slice_in_dim(pair_count, group_id * train_group, train_group)
        cumulative = jnp.cumsum(counts).astype(jnp.int32)
        live_pairs = cumulative[-1]
        slot_row = lax.dynamic_index_in_dim(pair_slot, group_id, 0, keepdims=False)
        owners = lax.dynamic_index_in_dim(slot_tile, group_id, 0, keepdims=False)

        def block_step(block_id, accumulated):
            position = block_id * reference_block + offsets
            in_range = position < live_pairs
            clipped = jnp.minimum(position, list_length - 1)
            local_tile = lax.optimization_barrier(jnp.sum((cumulative[None, :] <= clipped[:, None]).astype(jnp.int32), axis=1))
            local_tile = jnp.minimum(local_tile, train_group - 1)
            tile_ids = (group_id * train_group + local_tile).astype(jnp.int32)
            target = slot_row[clipped]
            test_ids = (target * test_group + owners[target]).astype(jnp.int32)
            kernel = wendland(test_points[test_ids], train_points[tile_ids])
            kernel = jnp.where(in_range[:, None, None], kernel, 0.0).astype(jnp.bfloat16)
            kernel = lax.optimization_barrier(kernel).astype(jnp.float32)
            weights = masked[tile_ids].astype(jnp.float32)
            contribution = jnp.einsum('bij,bjs->bis', kernel, weights)
            return accumulated.at[test_ids].add(contribution)
        block_count = (live_pairs + reference_block - 1) // reference_block
        return (lax.fori_loop(0, block_count, block_step, accumulated), None)
    accumulated = jnp.zeros((N_WIDE * test_group, TT, S), jnp.float32)
    accumulated, unused = lax.scan(group_step, accumulated, jnp.arange(N_WIDE, dtype=jnp.int32))
    test_live = jnp.arange(TT, dtype=jnp.int32)[None, :] < test_counts[:, None]
    update = jnp.where(test_live[:, :, None], accumulated, 0.0)
    return (prior.astype(jnp.float32) + update).astype(jnp.bfloat16)
```

```python
import functools

import jax
import jax.numpy as jnp
from jax import lax
from jax.experimental import pallas as pl
from jax.experimental.pallas import tpu as pltpu
from jax.sharding import PartitionSpec as P

f32, bf16, i32 = jnp.float32, jnp.bfloat16, jnp.int32
ROWS = 128
COLS = 512
BLOCK = 16
VMEM_LIMIT = 48 * 1024 * 1024
VMEM = pl.BlockSpec(memory_space=pltpu.VMEM)
SMEM = pl.BlockSpec(memory_space=pltpu.SMEM)


def split3(x):
    high = x.astype(bf16).astype(f32)
    rest = x - high
    mid = rest.astype(bf16).astype(f32)
    low = (rest - mid).astype(bf16).astype(f32)
    return high, mid, low


def prepare_kernel(
    narrow_id_ref, train_counts_ref, pair_count_ref, points_ref, weights_ref, pair_slot_ref,
    packed_weights_ref, packed_points_ref, packed_times_ref,
    wide_weights, raw_points,
):
    own_tiles, tile, columns = weights_ref.shape
    slots = packed_times_ref.shape[0]
    list_length = pair_slot_ref.shape[1]
    first_tile = narrow_id_ref[0] * own_tiles
    window = tile + 128
    positions = lax.broadcasted_iota(i32, (1, list_length), 1)
    named = pair_slot_ref[...]
    one_hot = (
        lax.broadcasted_iota(i32, (slots, list_length), 0) == jnp.broadcast_to(named, (slots, list_length))
    ).astype(f32)
    row8 = lax.broadcasted_iota(i32, (8, tile), 0)
    lane = lax.broadcasted_iota(i32, (8, window), 1)
    lane_slots = lax.broadcasted_iota(i32, (slots, window), 1)

    def skip(t, total):
        return total + pair_count_ref[t]

    first_pair = lax.fori_loop(0, first_tile, skip, jnp.int32(0))

    def step(t, carry):
        offset, pair = carry
        u = points_ref[first_tile + t] - 1.0
        square = jnp.sum(u * u, axis=0, keepdims=True)
        padded = jnp.concatenate([u, jnp.zeros((8 - u.shape[0], tile), f32)], axis=0)
        raw = jnp.where(
            row8 < 3, padded, jnp.where(row8 == 3, square, jnp.where(row8 == 4, 1.0, 0.0))
        )
        pair_end = pair + pair_count_ref[first_tile + t]
        inside = jnp.logical_and(positions >= pair, positions < pair_end)
        times = jnp.sum(jnp.where(inside, one_hot, 0.0), axis=1, keepdims=True)
        shift = lax.rem(offset, 128)
        base = pl.multiple_of(offset - shift, 128)
        rolled = pltpu.roll(
            jnp.concatenate([raw, jnp.zeros((8, 128), f32)], axis=1), shift, 1
        )
        spot = pl.ds(base, window)
        raw_points[:, spot] = jnp.where(lane >= shift, rolled, raw_points[:, spot])
        packed_times_ref[:, spot] = jnp.where(
            lane_slots >= shift, times, packed_times_ref[:, spot]
        )
        wide_weights[pl.ds(offset, tile), :] = weights_ref[t].astype(f32)
        return offset + train_counts_ref[first_tile + t], pair_end

    total, _ = lax.fori_loop(0, own_tiles, step, (jnp.int32(0), first_pair))
    shift = lax.rem(total, 128)
    base = pl.multiple_of(total - shift, 128)
    tail = COLS + 128
    spot = pl.ds(base, tail)
    raw_points[:, spot] = jnp.where(
        lax.broadcasted_iota(i32, (8, tail), 1) >= shift, 0.0, raw_points[:, spot]
    )
    packed_times_ref[:, spot] = jnp.where(
        lax.broadcasted_iota(i32, (slots, tail), 1) >= shift, 0.0, packed_times_ref[:, spot]
    )
    wide_weights[pl.ds(total, COLS), :] = jnp.zeros((COLS, columns), f32)

    def finish(c, carry):
        start = pl.multiple_of(c * COLS, COLS)
        high, mid, low = split3(raw_points[:, pl.ds(start, COLS)])
        packed_points_ref[:, pl.ds(start, COLS)] = jnp.concatenate(
            [high, mid, high, mid, low, high], axis=0
        ).astype(bf16)
        packed_weights_ref[pl.ds(start, COLS), :] = wide_weights[pl.ds(start, COLS), :].astype(bf16)
        return carry

    lax.fori_loop(0, (total + COLS - 1) // COLS, finish, 0)


def prepare(narrow_id, train_counts, pair_count, points, weights, pair_slot, slots):
    own_tiles, tile, columns = weights.shape
    length = own_tiles * tile + COLS + 128
    return pl.pallas_call(
        prepare_kernel,
        out_shape=(
            jax.ShapeDtypeStruct((length, columns), bf16),
            jax.ShapeDtypeStruct((48, length), bf16),
            jax.ShapeDtypeStruct((slots, length), f32),
        ),
        in_specs=[SMEM, SMEM, SMEM, VMEM, VMEM, VMEM],
        out_specs=(VMEM, VMEM, VMEM),
        scratch_shapes=[pltpu.VMEM((length, columns), f32), pltpu.VMEM((8, length), f32)],
        compiler_params=pltpu.CompilerParams(vmem_limit_bytes=VMEM_LIMIT),
        cost_estimate=pl.CostEstimate(flops=40_000_000, bytes_accessed=4_000_000, transcendentals=0),
        name="prepare",
    )(narrow_id, train_counts, pair_count, points, weights, pair_slot)


def main_kernel(
    narrow_id_ref, train_counts_ref, received_ref, packed_weights_ref, packed_points_ref, packed_times_ref,
    partial_ref,
    rows_ref, sums_ref, block_slot, slot_row,
):
    slots, test_tile, columns = partial_ref.shape
    senders = received_ref.shape[0] // slots
    own_tiles = train_counts_ref.shape[0] // senders
    first_tile = narrow_id_ref[0] * own_tiles
    total = lax.fori_loop(
        0, own_tiles, lambda t, a: a + train_counts_ref[first_tile + t], jnp.int32(0)
    )
    row8 = lax.broadcasted_iota(i32, (8, test_tile), 0)
    per_slot = test_tile // BLOCK

    def place(g, offset):
        got = received_ref[g * senders]
        for s in range(1, senders):
            got = got + received_ref[g * senders + s]
        count = jnp.max(got[3:4, :]).astype(i32)
        v = jnp.concatenate([got, got], axis=0) - 1.0
        square = jnp.sum(jnp.where(row8 < 3, v * v, 0.0), axis=0, keepdims=True)
        raw = jnp.where(
            row8 < 3, -2.0 * v, jnp.where(row8 == 3, 1.0, jnp.where(row8 == 4, square, 0.0))
        )
        high, mid, low = split3(raw)
        operand = jnp.concatenate([high, high, mid, mid, high, low], axis=0)
        rows_ref[pl.ds(pl.multiple_of(offset * BLOCK, BLOCK), test_tile), :] = operand.T.astype(bf16)
        slot_row[g] = offset
        for b in range(per_slot):
            block_slot[offset + b] = g
        return offset + (count + BLOCK - 1) // BLOCK

    blocks = lax.fori_loop(0, slots, place, jnp.int32(0))
    per_tile = ROWS // BLOCK
    for b in range(per_tile):
        block_slot[blocks + b] = 0
    row_tiles = (blocks + per_tile - 1) // per_tile
    col_tiles = (total + COLS - 1) // COLS

    def row_step(r, carry):
        row_start = pl.multiple_of(r * ROWS, ROWS)
        left = rows_ref[pl.ds(row_start, ROWS), :]

        def col_step(c, acc):
            col_start = pl.multiple_of(c * COLS, COLS)
            d2 = jnp.dot(left, packed_points_ref[:, pl.ds(col_start, COLS)], preferred_element_type=f32)
            pieces = []
            for b in range(per_tile):
                times = packed_times_ref[pl.ds(block_slot[r * per_tile + b], 1), pl.ds(col_start, COLS)]
                part = jnp.maximum(d2[b * BLOCK : (b + 1) * BLOCK], 1e-30)
                falloff = jnp.maximum(1.0 - part * lax.rsqrt(part), 0.0)
                second = falloff * falloff
                pieces.append((second * second * (5.0 * times - (4.0 * times) * falloff)).astype(bf16))
            kernel = jnp.concatenate(pieces, axis=0)
            return acc + jnp.dot(kernel, packed_weights_ref[pl.ds(col_start, COLS), :], preferred_element_type=f32)

        sums_ref[pl.ds(row_start, ROWS), :] = lax.fori_loop(
            0, col_tiles, col_step, jnp.zeros((ROWS, columns), f32)
        )
        return carry

    lax.fori_loop(0, row_tiles, row_step, 0)

    def give(g, carry):
        start = pl.multiple_of(slot_row[g] * BLOCK, BLOCK)
        partial_ref[g] = sums_ref[pl.ds(start, test_tile), :].astype(bf16)
        return carry

    lax.fori_loop(0, slots, give, 0)


def partials(narrow_id, train_counts, received, packed, slots, columns):
    test_tile = received.shape[2]
    height = slots * test_tile
    return pl.pallas_call(
        main_kernel,
        out_shape=jax.ShapeDtypeStruct((slots, test_tile, columns), bf16),
        in_specs=[SMEM, SMEM, VMEM, VMEM, VMEM, VMEM],
        out_specs=VMEM,
        scratch_shapes=[
            pltpu.VMEM((height, 48), bf16),
            pltpu.VMEM((height, columns), f32),
            pltpu.SMEM((height // BLOCK + ROWS // BLOCK,), i32),
            pltpu.SMEM((slots,), i32),
        ],
        compiler_params=pltpu.CompilerParams(vmem_limit_bytes=VMEM_LIMIT),
        cost_estimate=pl.CostEstimate(flops=3_000_000_000, bytes_accessed=4_000_000, transcendentals=8_000_000),
        name="partials",
    )(narrow_id, train_counts, received, *packed)


def collect_kernel(first_ref, owner_ref, collected_ref, out_ref):
    sources = collected_ref.shape[0]
    tiles = out_ref.shape[0]
    acc = [jnp.zeros(out_ref.shape[1:], f32) for _ in range(tiles)]
    for w in range(sources):
        block = collected_ref[w].astype(f32)
        tile = owner_ref[w] - first_ref[0]
        for t in range(tiles):
            acc[t] = acc[t] + jnp.where(tile == t, block, 0.0)
    for t in range(tiles):
        out_ref[t] = acc[t].astype(out_ref.dtype)


def collect(first, owners, collected, tiles, dtype):
    return pl.pallas_call(
        collect_kernel,
        out_shape=jax.ShapeDtypeStruct((tiles,) + collected.shape[1:], dtype),
        in_specs=[SMEM, SMEM, VMEM],
        out_specs=VMEM,
        compiler_params=pltpu.CompilerParams(vmem_limit_bytes=VMEM_LIMIT),
        cost_estimate=pl.CostEstimate(flops=1_000_000, bytes_accessed=700_000, transcendentals=0),
        name="collect",
    )(first, owners, collected)


def body(
    train_points, train_weights, train_counts, test_points, prior, test_counts, pair_count, pair_slot, slot_tile
):
    narrow_size = lax.axis_size("narrow")
    wide_size = lax.axis_size("wide")
    narrow_id = lax.axis_index("narrow")
    wide_id = lax.axis_index("wide")
    own_tests = test_points.shape[0]
    slots = slot_tile.shape[0]
    columns = train_weights.shape[2]

    wanted = lax.dynamic_index_in_dim(slot_tile, wide_id, 1, keepdims=False) - narrow_id * own_tests
    payload = jnp.concatenate(
        [
            test_points,
            jnp.broadcast_to(
                test_counts.astype(f32)[:, None, None], (own_tests, 1, test_points.shape[2])
            ),
        ],
        axis=1,
    )
    outgoing = jnp.zeros((wide_size,) + payload.shape[1:], f32)
    for t in range(own_tests):
        outgoing = jnp.where((wanted == t)[:, None, None], payload[t][None], outgoing)
    outgoing = jnp.broadcast_to(
        outgoing[:, None], (wide_size, narrow_size) + payload.shape[1:]
    ).reshape((wide_size * narrow_size,) + payload.shape[1:])
    received = lax.all_to_all(outgoing, ("wide", "narrow"), 0, 0, tiled=True)

    nid = narrow_id.astype(i32)[None]
    packed = prepare(nid, train_counts, pair_count, train_points, train_weights, pair_slot, slots)
    partial_value = partials(nid, train_counts, received, packed, slots, columns)
    collected = lax.all_to_all(partial_value, "wide", 0, 0, tiled=True)
    owners = lax.dynamic_index_in_dim(slot_tile, wide_id, 1, keepdims=False)
    arrived = []
    for k in range(1, narrow_size):
        target = lax.rem(narrow_id + k, narrow_size)
        sent = collect((target * own_tests).astype(i32)[None], owners, collected, own_tests, bf16)
        arrived.append(
            lax.ppermute(sent, "narrow", [(i, (i + k) % narrow_size) for i in range(narrow_size)])
        )
    owned = collect((narrow_id * own_tests).astype(i32)[None], owners, collected, own_tests, f32)
    for part in arrived:
        owned = owned + part.astype(f32)
    test_live = jnp.arange(prior.shape[1], dtype=i32)[None, :] < test_counts[:, None]
    update = jnp.where(test_live[:, :, None], owned, 0.0)
    return (prior.astype(f32) + update).astype(bf16)


def solution(mesh):
    return jax.shard_map(
        body,
        mesh=mesh,
        in_specs=(
            P("wide", None, None),
            P(("wide", "narrow"), None, None),
            P("wide"),
            P(("wide", "narrow"), None, None),
            P(("wide", "narrow"), None, None),
            P(("wide", "narrow")),
            P("wide"),
            P("wide", None),
            P(),
        ),
        out_specs=P(("wide", "narrow"), None, None),
        check_vma=False,
    )
```

```python
import functools
import math

import jax
import jax.numpy as jnp
from jax import lax
from jax.experimental import pallas as pl
from jax.experimental.pallas import tpu as pltpu
from jax.sharding import PartitionSpec as P

f32, bf16, i32 = jnp.float32, jnp.bfloat16, jnp.int32
COLS = 256
BLOCK = 16
PART = 8
PARTS = 4
DEPTH = 256
SCALE = 4.0**0.2
VMEM_LIMIT = 48 * 1024 * 1024
VMEM = pl.BlockSpec(memory_space=pltpu.VMEM)
SMEM = pl.BlockSpec(memory_space=pltpu.SMEM)
HBM = pl.BlockSpec(memory_space=pltpu.HBM)


def split3(x):
    high = x.astype(bf16).astype(f32)
    rest = x - high
    mid = rest.astype(bf16).astype(f32)
    low = (rest - mid).astype(bf16).astype(f32)
    return high, mid, low


def stay(*arrays):
    return [pltpu.with_memory_space_constraint(array, pltpu.HBM) for array in arrays]


def offer_kernel(slot_tile_hbm, test_counts_hbm, test_points_hbm, offer_ref, slot_tile, test_counts, points, sems):
    axes, own_tests, test_tile = points.shape
    senders = offer_ref.shape[0]
    wide_size = slot_tile.shape[0]
    copies = [
        pltpu.make_async_copy(source, target, sems.at[i])
        for i, (source, target) in enumerate(
            ((slot_tile_hbm, slot_tile), (test_counts_hbm, test_counts), (test_points_hbm, points))
        )
    ]
    for copy in copies:
        copy.start()
    first = lax.axis_index("narrow") * own_tests
    group = lax.axis_index("wide")
    for copy in copies:
        copy.wait()
    payloads = [
        jnp.concatenate(
            [
                *(points[axis, t : t + 1, :] for axis in range(axes)),
                jnp.full((1, test_tile), test_counts[t].astype(f32), f32),
            ],
            axis=0,
        )
        for t in range(own_tests)
    ]
    narrow_size = senders // wide_size

    def step(w, carry):
        wanted = slot_tile[w, group] - first
        chosen = jnp.zeros((axes + 1, test_tile), f32)
        for t in range(own_tests):
            chosen = jnp.where(wanted == t, payloads[t], chosen)
        for n in range(narrow_size):
            offer_ref[w * narrow_size + n] = chosen
        return carry

    lax.fori_loop(0, wide_size, step, 0, unroll=4)


def offer(slot_tile, test_counts, test_points, senders):
    axes, own_tests, test_tile = test_points.shape
    return pl.pallas_call(
        offer_kernel,
        out_shape=jax.ShapeDtypeStruct((senders, axes + 1, test_tile), f32),
        in_specs=[HBM, HBM, HBM],
        out_specs=VMEM,
        scratch_shapes=[
            pltpu.SMEM(slot_tile.shape, i32),
            pltpu.SMEM(test_counts.shape, i32),
            pltpu.VMEM(test_points.shape, f32),
            pltpu.SemaphoreType.DMA((3,)),
        ],
        compiler_params=pltpu.CompilerParams(vmem_limit_bytes=VMEM_LIMIT),
        cost_estimate=pl.CostEstimate(flops=100_000, bytes_accessed=100_000, transcendentals=0),
        name="offer",
    )(*stay(slot_tile, test_counts, test_points))


def prepare_kernel(
    train_counts_hbm, pair_count_hbm, points_hbm, weights_hbm, pair_slot_hbm,
    packed_weights_ref, packed_points_ref, packed_times_ref,
    wide_weights, raw_points, train_counts_ref, pair_count_ref, points_ref, weights_ref, pair_slot_ref, sems,
):
    own_tiles, tile, columns = weights_ref.shape
    copies = [
        pltpu.make_async_copy(source, target, sems.at[i])
        for i, (source, target) in enumerate(
            (
                (train_counts_hbm, train_counts_ref),
                (pair_count_hbm, pair_count_ref),
                (points_hbm, points_ref),
                (weights_hbm, weights_ref),
                (pair_slot_hbm, pair_slot_ref),
            )
        )
    ]
    for copy in copies:
        copy.start()
    for copy in copies:
        copy.wait()
    slots = packed_times_ref.shape[0]
    list_length = pair_slot_ref.shape[1]
    first_tile = lax.axis_index("narrow") * own_tiles
    window = tile + 128
    positions = lax.broadcasted_iota(i32, (1, list_length), 1)
    named = pair_slot_ref[...]
    one_hot = (
        lax.broadcasted_iota(i32, (slots, list_length), 0) == jnp.broadcast_to(named, (slots, list_length))
    ).astype(f32)
    row8 = lax.broadcasted_iota(i32, (8, tile), 0)
    lane = lax.broadcasted_iota(i32, (8, window), 1)
    lane_slots = lax.broadcasted_iota(i32, (slots, window), 1)

    def skip(t, total):
        return total + pair_count_ref[t]

    first_pair = lax.fori_loop(0, first_tile, skip, jnp.int32(0))

    def step(t, carry):
        offset, pair = carry
        u = [
            SCALE * (points_ref[axis, pl.ds(first_tile + t, 1), :] - 1.0)
            for axis in range(points_ref.shape[0])
        ]
        square = u[0] * u[0] + u[1] * u[1] + u[2] * u[2]
        raw = jnp.where(row8 == 4, 1.0, 0.0)
        for row, value in enumerate((*u, square)):
            raw = jnp.where(row8 == row, value, raw)
        pair_end = pair + pair_count_ref[first_tile + t]
        inside = jnp.logical_and(positions >= pair, positions < pair_end)
        times = jnp.sum(jnp.where(inside, one_hot, 0.0), axis=1, keepdims=True)
        shift = lax.rem(offset, 128)
        base = pl.multiple_of(offset - shift, 128)
        rolled = pltpu.roll(
            jnp.concatenate([raw, jnp.zeros((8, 128), f32)], axis=1), shift, 1
        )
        spot = pl.ds(base, window)
        raw_points[:, spot] = jnp.where(lane >= shift, rolled, raw_points[:, spot])
        packed_times_ref[:, spot] = jnp.where(
            lane_slots >= shift, times, packed_times_ref[:, spot]
        )
        wide_weights[pl.ds(offset, tile), :] = weights_ref[t].astype(f32)
        return offset + train_counts_ref[first_tile + t], pair_end

    total, _ = lax.fori_loop(0, own_tiles, step, (jnp.int32(0), first_pair))
    shift = lax.rem(total, 128)
    base = pl.multiple_of(total - shift, 128)
    tail = COLS + 128
    spot = pl.ds(base, tail)
    raw_points[:, spot] = jnp.where(
        lax.broadcasted_iota(i32, (8, tail), 1) >= shift, 0.0, raw_points[:, spot]
    )
    packed_times_ref[:, spot] = jnp.where(
        lax.broadcasted_iota(i32, (slots, tail), 1) >= shift, 0.0, packed_times_ref[:, spot]
    )
    wide_weights[pl.ds(total, COLS), :] = jnp.zeros((COLS, columns), f32)

    def finish(c, carry):
        start = pl.multiple_of(c * COLS, COLS)
        high, mid, low = split3(raw_points[:, pl.ds(start, COLS)])
        packed_points_ref[:, pl.ds(start, COLS)] = jnp.concatenate(
            [high, mid, high, mid, low, high], axis=0
        ).astype(bf16)
        packed_weights_ref[pl.ds(start, COLS), :] = wide_weights[pl.ds(start, COLS), :].astype(bf16)
        return carry

    lax.fori_loop(0, (total + COLS - 1) // COLS, finish, 0)


def prepare(train_counts, pair_count, points, weights, pair_slot, slots):
    own_tiles, tile, columns = weights.shape
    length = own_tiles * tile + COLS + 128
    return pl.pallas_call(
        prepare_kernel,
        out_shape=(
            jax.ShapeDtypeStruct((length, columns), bf16),
            jax.ShapeDtypeStruct((48, length), bf16),
            jax.ShapeDtypeStruct((slots, length), f32),
        ),
        in_specs=[HBM] * 5,
        out_specs=(VMEM, VMEM, VMEM),
        scratch_shapes=[
            pltpu.VMEM((length, columns), f32),
            pltpu.VMEM((8, length), f32),
            pltpu.SMEM(train_counts.shape, i32),
            pltpu.SMEM(pair_count.shape, i32),
            pltpu.VMEM(points.shape, f32),
            pltpu.VMEM(weights.shape, bf16),
            pltpu.VMEM(pair_slot.shape, i32),
            pltpu.SemaphoreType.DMA((5,)),
        ],
        compiler_params=pltpu.CompilerParams(vmem_limit_bytes=VMEM_LIMIT),
        cost_estimate=pl.CostEstimate(flops=40_000_000, bytes_accessed=4_000_000, transcendentals=0),
        name="prepare",
    )(*stay(train_counts, pair_count, points, weights, pair_slot))


def main_kernel(
    train_counts_ref, received_ref, packed_weights_ref, packed_points_ref, packed_times_ref,
    partial_ref,
    rows_ref, sums_ref, block_slot, slot_row,
):
    slots, test_tile, columns = partial_ref.shape
    senders = received_ref.shape[0] // slots
    own_tiles = train_counts_ref.shape[0] // senders
    depth = packed_points_ref.shape[0]
    first_tile = lax.axis_index("narrow") * own_tiles
    total = lax.fori_loop(
        0, own_tiles, lambda t, a: a + train_counts_ref[first_tile + t], jnp.int32(0)
    )
    row8 = lax.broadcasted_iota(i32, (8, test_tile), 0)
    per_slot = test_tile // BLOCK
    rows_ref[...] = jnp.zeros(rows_ref.shape, bf16)
    sums_ref[...] = jnp.zeros(sums_ref.shape, f32)
    together = math.gcd(slots, 16)

    def place(step, offset):
        operands, counts = [], []
        for i in range(together):
            g = step * together + i
            got = received_ref[g * senders]
            for s in range(1, senders):
                got = got + received_ref[g * senders + s]
            counts.append(jnp.max(got[3:4, :]).astype(i32))
            v = SCALE * (jnp.concatenate([got, got], axis=0) - 1.0)
            square = jnp.sum(jnp.where(row8 < 3, v * v, 0.0), axis=0, keepdims=True)
            raw = jnp.where(
                row8 < 3, -2.0 * v, jnp.where(row8 == 3, 1.0, jnp.where(row8 == 4, square, 0.0))
            )
            high, mid, low = split3(raw)
            operands.append(
                jnp.concatenate([high, high, mid, mid, high, low], axis=0).T.astype(bf16)
            )
        for i in range(together):
            g = step * together + i
            start = pl.multiple_of(offset * BLOCK, BLOCK)
            rows_ref[pl.ds(start, test_tile), 0:depth] = operands[i]
            slot_row[g] = offset
            for b in range(per_slot):
                block_slot[offset + b] = g
            offset = offset + (counts[i] + BLOCK - 1) // BLOCK
        return offset

    blocks = lax.fori_loop(0, slots // together, place, jnp.int32(0))
    for b in range(2 * PART):
        block_slot[blocks + b] = 0
    parts = (blocks + PART - 1) // PART
    parts = jnp.where(parts < 3, 3, jnp.where(parts == 5, 6, parts))
    steps = (parts + PARTS - 1) // PARTS
    shorter = PARTS * steps - parts
    longer = steps - shorter
    col_tiles = (total + COLS - 1) // COLS
    nothing = jnp.zeros((BLOCK, DEPTH), bf16)
    ring = PARTS * PART

    def with_accumulators(*accs):
        square_accs, sum_accs = accs[: ring + 1], accs[ring + 1 :]
        for acc in accs:
            pltpu.matmul_pop(acc)

        def load_points(c):
            rows = packed_points_ref[:, pl.ds(pl.multiple_of(c * COLS, COLS), COLS)]
            pltpu.matmul_push_rhs(
                jnp.concatenate([rows, jnp.zeros((DEPTH - depth, COLS), bf16)], axis=0), 0, 0
            )
            pltpu.matmul_acc_lhs(square_accs[ring], nothing, load_staged_rhs=0)

        def load_weights(c):
            rows = packed_weights_ref[pl.ds(pl.multiple_of(c * COLS, COLS), COLS), :]
            pltpu.matmul_push_rhs(
                jnp.concatenate([rows, jnp.zeros((COLS, DEPTH - columns), bf16)], axis=1), 0, 1
            )
            pltpu.matmul_acc_lhs(sum_accs[ring], nothing, load_staged_rhs=0)

        def block_rows(part, b):
            return pl.ds(pl.multiple_of(part * (PART * BLOCK) + b * BLOCK, BLOCK), BLOCK)

        def start_squares(part, b):
            rows = rows_ref[block_rows(part, b), :]
            pltpu.matmul_acc_lhs(
                square_accs[b],
                jnp.concatenate([rows, jnp.zeros((BLOCK, DEPTH - rows.shape[1]), bf16)], axis=1),
            )

        def gather_sums(part, b):
            rows = block_rows(part, b)
            sums_ref[rows, :] = sums_ref[rows, :] + pltpu.matmul_pop(sum_accs[b])[:, :columns]

        def evaluate(c, part, count, after, before):
            col = pl.ds(pl.multiple_of(c * COLS, COLS), COLS)
            for b in range(ring):
                square = pltpu.matmul_pop(square_accs[b])
                start_squares(after, b)
                gather_sums(before, b)
                if b < count * PART:
                    square = jnp.maximum(square, 1e-30)
                    times = packed_times_ref[pl.ds(block_slot[part * PART + b], 1), col]
                    falloff = jnp.maximum(SCALE - square * lax.rsqrt(square), 0.0)
                    second = falloff * falloff
                    kernel = (second * second * (1.25 * SCALE - falloff) * times).astype(bf16)
                    pltpu.matmul_acc_lhs(sum_accs[b], kernel)

        def last_step(c, before, count):
            load_points(c + 1)
            evaluate(c, parts - count, count, 0, before)
            load_weights(c + 1)

        def col_step(c, before):
            def long_step(q, before):
                part = PARTS * q
                evaluate(c, part, PARTS, part + PARTS, before)
                return part

            def short_step(q, before):
                part = PARTS * longer + (PARTS - 1) * q
                evaluate(c, part, PARTS - 1, part + (PARTS - 1), before)
                return part

            before = lax.fori_loop(0, longer - (shorter == 0).astype(i32), long_step, before)
            before = lax.fori_loop(0, shorter - 1, short_step, before)
            pl.when(shorter == 0)(functools.partial(last_step, c, before, PARTS))
            pl.when(shorter > 0)(functools.partial(last_step, c, before, PARTS - 1))
            return parts - jnp.where(shorter == 0, PARTS, PARTS - 1)

        load_points(jnp.int32(0))
        load_weights(jnp.int32(0))
        for b in range(ring):
            start_squares(jnp.int32(0), b)
        before = lax.fori_loop(0, col_tiles, col_step, jnp.int32(0))
        for b in range(ring):
            gather_sums(before, b)
            pltpu.matmul_pop(square_accs[b])
        pltpu.matmul_pop(square_accs[ring])
        pltpu.matmul_pop(sum_accs[ring])

    pl.run_scoped(
        with_accumulators,
        *[pltpu.ACC(mxu)((BLOCK, DEPTH), f32) for mxu in range(2) for _ in range(ring + 1)],
    )

    def give(step, carry):
        for i in range(together):
            g = step * together + i
            start = pl.multiple_of(slot_row[g] * BLOCK, BLOCK)
            partial_ref[g] = sums_ref[pl.ds(start, test_tile), :].astype(bf16)
        return carry

    lax.fori_loop(0, slots // together, give, 0)


def partials(train_counts, received, packed, slots, columns):
    test_tile = received.shape[2]
    step_rows = PARTS * PART * BLOCK
    height = max(slots * test_tile, 6 * PART * BLOCK) + step_rows
    return pl.pallas_call(
        main_kernel,
        out_shape=jax.ShapeDtypeStruct((slots, test_tile, columns), bf16),
        in_specs=[SMEM, VMEM, VMEM, VMEM, VMEM],
        out_specs=VMEM,
        scratch_shapes=[
            pltpu.VMEM((height, 128), bf16),
            pltpu.VMEM((height, columns), f32),
            pltpu.SMEM((height // BLOCK,), i32),
            pltpu.SMEM((slots,), i32),
        ],
        compiler_params=pltpu.CompilerParams(vmem_limit_bytes=VMEM_LIMIT),
        cost_estimate=pl.CostEstimate(flops=3_000_000_000, bytes_accessed=4_000_000, transcendentals=8_000_000),
        name="partials",
    )(train_counts, received, *packed)


def collect_kernel(shift, slot_tile_ref, collected_ref, out_ref):
    sources = collected_ref.shape[0]
    tiles = out_ref.shape[0]
    group = lax.axis_index("wide")
    first = lax.rem(lax.axis_index("narrow") + shift, lax.axis_size("narrow")) * tiles
    acc = [jnp.zeros(out_ref.shape[1:], f32) for _ in range(tiles)]
    for w in range(sources):
        block = collected_ref[w].astype(f32)
        tile = slot_tile_ref[w, group] - first
        for t in range(tiles):
            acc[t] = acc[t] + jnp.where(tile == t, block, 0.0)
    for t in range(tiles):
        out_ref[t] = acc[t].astype(out_ref.dtype)


def collect(shift, slot_tile, collected, tiles, dtype):
    return pl.pallas_call(
        functools.partial(collect_kernel, shift),
        out_shape=jax.ShapeDtypeStruct((tiles,) + collected.shape[1:], dtype),
        in_specs=[SMEM, VMEM],
        out_specs=VMEM,
        compiler_params=pltpu.CompilerParams(vmem_limit_bytes=VMEM_LIMIT),
        cost_estimate=pl.CostEstimate(flops=1_000_000, bytes_accessed=700_000, transcendentals=0),
        name="collect",
    )(slot_tile, collected)


def body(
    train_points, train_weights, train_counts, test_points, prior, test_counts, pair_count, pair_slot, slot_tile
):
    narrow_size = lax.axis_size("narrow")
    own_tests = test_points.shape[0]
    slots = slot_tile.shape[0]
    columns = train_weights.shape[2]
    offered = offer(slot_tile, test_counts, jnp.transpose(test_points, (1, 0, 2)), slots * narrow_size)
    received = lax.all_to_all(offered, ("wide", "narrow"), 0, 0, tiled=True)
    packed = prepare(
        train_counts, pair_count, jnp.transpose(train_points, (1, 0, 2)), train_weights, pair_slot, slots
    )
    partial_value = partials(train_counts, received, packed, slots, columns)
    collected = lax.all_to_all(partial_value, "wide", 0, 0, tiled=True)
    arrived = []
    for k in range(1, narrow_size):
        sent = collect(k, slot_tile, collected, own_tests, bf16)
        arrived.append(
            lax.ppermute(sent, "narrow", [(i, (i + k) % narrow_size) for i in range(narrow_size)])
        )
    owned = collect(0, slot_tile, collected, own_tests, f32)
    for part in arrived:
        owned = owned + part.astype(f32)
    test_live = jnp.arange(prior.shape[1], dtype=i32)[None, :] < test_counts[:, None]
    update = jnp.where(test_live[:, :, None], owned, 0.0)
    return (prior.astype(f32) + update).astype(bf16)


def solution(mesh):
    return jax.shard_map(
        body,
        mesh=mesh,
        in_specs=(
            P("wide", None, None),
            P(("wide", "narrow"), None, None),
            P("wide"),
            P(("wide", "narrow"), None, None),
            P(("wide", "narrow"), None, None),
            P(("wide", "narrow")),
            P("wide"),
            P("wide", None),
            P(),
        ),
        out_specs=P(("wide", "narrow"), None, None),
        check_vma=False,
    )
```

```python
import functools
import math

import jax
import jax.numpy as jnp
from jax import lax
from jax.experimental import pallas as pl
from jax.experimental.pallas import tpu as pltpu
from jax.sharding import PartitionSpec as P

f32, bf16, i32 = jnp.float32, jnp.bfloat16, jnp.int32
COLS = 256
BLOCK = 16
PART = 8
PARTS = 4
DEPTH = 256
SCALE = 4.0**0.2
VMEM_LIMIT = 32 * 1024 * 1024
VMEM = pl.BlockSpec(memory_space=pltpu.VMEM)
SMEM = pl.BlockSpec(memory_space=pltpu.SMEM)
HBM = pl.BlockSpec(memory_space=pltpu.HBM)


def split3(x):
    high = x.astype(bf16).astype(f32)
    rest = x - high
    mid = rest.astype(bf16).astype(f32)
    low = (rest - mid).astype(bf16).astype(f32)
    return high, mid, low


def stay(*arrays):
    return [pltpu.with_memory_space_constraint(array, pltpu.HBM) for array in arrays]


def offer_kernel(slot_tile_hbm, test_counts_hbm, test_points_hbm, offer_ref, slot_tile, test_counts, points, sems):
    axes, own_tests, test_tile = points.shape
    senders = offer_ref.shape[0]
    wide_size = slot_tile.shape[0]
    copies = [
        pltpu.make_async_copy(source, target, sems.at[i])
        for i, (source, target) in enumerate(
            ((slot_tile_hbm, slot_tile), (test_counts_hbm, test_counts), (test_points_hbm, points))
        )
    ]
    for copy in copies:
        copy.start()
    first = lax.axis_index("narrow") * own_tests
    group = lax.axis_index("wide")
    for copy in copies:
        copy.wait()
    payloads = [
        jnp.concatenate(
            [
                *(points[axis, t : t + 1, :] for axis in range(axes)),
                jnp.full((1, test_tile), test_counts[t].astype(f32), f32),
            ],
            axis=0,
        )
        for t in range(own_tests)
    ]
    narrow_size = senders // wide_size

    def step(w, carry):
        wanted = slot_tile[w, group] - first
        chosen = jnp.zeros((axes + 1, test_tile), f32)
        for t in range(own_tests):
            chosen = jnp.where(wanted == t, payloads[t], chosen)
        for n in range(narrow_size):
            offer_ref[w * narrow_size + n] = chosen
        return carry

    lax.fori_loop(0, wide_size, step, 0, unroll=4)


def offer(slot_tile, test_counts, test_points, senders):
    axes, own_tests, test_tile = test_points.shape
    return pl.pallas_call(
        offer_kernel,
        out_shape=jax.ShapeDtypeStruct((senders, axes + 1, test_tile), f32),
        in_specs=[HBM, HBM, HBM],
        out_specs=VMEM,
        scratch_shapes=[
            pltpu.SMEM(slot_tile.shape, i32),
            pltpu.SMEM(test_counts.shape, i32),
            pltpu.VMEM(test_points.shape, f32),
            pltpu.SemaphoreType.DMA((3,)),
        ],
        compiler_params=pltpu.CompilerParams(vmem_limit_bytes=VMEM_LIMIT),
        cost_estimate=pl.CostEstimate(flops=100_000, bytes_accessed=100_000, transcendentals=0),
        name="offer",
    )(*stay(slot_tile, test_counts, test_points))


def prepare_kernel(
    train_counts_hbm, pair_count_hbm, points_hbm, weights_hbm, pair_slot_hbm,
    packed_weights_ref, packed_points_ref, packed_times_ref,
    wide_weights, raw_points, train_counts_ref, pair_count_ref, points_ref, weights_ref, pair_slot_ref, sems,
):
    own_tiles, tile, columns = weights_ref.shape
    copies = [
        pltpu.make_async_copy(source, target, sems.at[i])
        for i, (source, target) in enumerate(
            (
                (train_counts_hbm, train_counts_ref),
                (pair_count_hbm, pair_count_ref),
                (points_hbm, points_ref),
                (weights_hbm, weights_ref),
                (pair_slot_hbm, pair_slot_ref),
            )
        )
    ]
    for copy in copies:
        copy.start()
    for copy in copies:
        copy.wait()
    slots = packed_times_ref.shape[0]
    list_length = pair_slot_ref.shape[1]
    first_tile = lax.axis_index("narrow") * own_tiles
    window = tile + 128
    positions = lax.broadcasted_iota(i32, (1, list_length), 1)
    named = pair_slot_ref[...]
    one_hot = (
        lax.broadcasted_iota(i32, (slots, list_length), 0) == jnp.broadcast_to(named, (slots, list_length))
    ).astype(f32)
    row8 = lax.broadcasted_iota(i32, (8, tile), 0)
    lane = lax.broadcasted_iota(i32, (8, window), 1)
    lane_slots = lax.broadcasted_iota(i32, (slots, window), 1)

    def skip(t, total):
        return total + pair_count_ref[t]

    first_pair = lax.fori_loop(0, first_tile, skip, jnp.int32(0))

    def step(t, carry):
        offset, pair = carry
        u = [
            SCALE * (points_ref[axis, pl.ds(first_tile + t, 1), :] - 1.0)
            for axis in range(points_ref.shape[0])
        ]
        square = u[0] * u[0] + u[1] * u[1] + u[2] * u[2]
        raw = jnp.where(row8 == 4, 1.0, 0.0)
        for row, value in enumerate((*u, square)):
            raw = jnp.where(row8 == row, value, raw)
        pair_end = pair + pair_count_ref[first_tile + t]
        inside = jnp.logical_and(positions >= pair, positions < pair_end)
        times = jnp.sum(jnp.where(inside, one_hot, 0.0), axis=1, keepdims=True)
        shift = lax.rem(offset, 128)
        base = pl.multiple_of(offset - shift, 128)
        rolled = pltpu.roll(
            jnp.concatenate([raw, jnp.zeros((8, 128), f32)], axis=1), shift, 1
        )
        spot = pl.ds(base, window)
        raw_points[:, spot] = jnp.where(lane >= shift, rolled, raw_points[:, spot])
        packed_times_ref[:, spot] = jnp.where(
            lane_slots >= shift, times, packed_times_ref[:, spot]
        )
        wide_weights[pl.ds(offset, tile), :] = weights_ref[t].astype(f32)
        return offset + train_counts_ref[first_tile + t], pair_end

    total, _ = lax.fori_loop(0, own_tiles, step, (jnp.int32(0), first_pair))
    shift = lax.rem(total, 128)
    base = pl.multiple_of(total - shift, 128)
    tail = COLS + 128
    spot = pl.ds(base, tail)
    raw_points[:, spot] = jnp.where(
        lax.broadcasted_iota(i32, (8, tail), 1) >= shift, 0.0, raw_points[:, spot]
    )
    packed_times_ref[:, spot] = jnp.where(
        lax.broadcasted_iota(i32, (slots, tail), 1) >= shift, 0.0, packed_times_ref[:, spot]
    )
    wide_weights[pl.ds(total, COLS), :] = jnp.zeros((COLS, columns), f32)

    def finish(c, carry):
        start = pl.multiple_of(c * COLS, COLS)
        high, mid, low = split3(raw_points[:, pl.ds(start, COLS)])
        packed_points_ref[:, pl.ds(start, COLS)] = jnp.concatenate(
            [high, mid, high, mid, low, high], axis=0
        ).astype(bf16)
        packed_weights_ref[pl.ds(start, COLS), :] = wide_weights[pl.ds(start, COLS), :].astype(bf16)
        return carry

    lax.fori_loop(0, (total + COLS - 1) // COLS, finish, 0)


def prepare(train_counts, pair_count, points, weights, pair_slot, slots):
    own_tiles, tile, columns = weights.shape
    length = own_tiles * tile + COLS + 128
    return pl.pallas_call(
        prepare_kernel,
        out_shape=(
            jax.ShapeDtypeStruct((length, columns), bf16),
            jax.ShapeDtypeStruct((48, length), bf16),
            jax.ShapeDtypeStruct((slots, length), f32),
        ),
        in_specs=[HBM] * 5,
        out_specs=(VMEM, VMEM, VMEM),
        scratch_shapes=[
            pltpu.VMEM((length, columns), f32),
            pltpu.VMEM((8, length), f32),
            pltpu.SMEM(train_counts.shape, i32),
            pltpu.SMEM(pair_count.shape, i32),
            pltpu.VMEM(points.shape, f32),
            pltpu.VMEM(weights.shape, bf16),
            pltpu.VMEM(pair_slot.shape, i32),
            pltpu.SemaphoreType.DMA((5,)),
        ],
        compiler_params=pltpu.CompilerParams(vmem_limit_bytes=VMEM_LIMIT),
        cost_estimate=pl.CostEstimate(flops=40_000_000, bytes_accessed=4_000_000, transcendentals=0),
        name="prepare",
    )(*stay(train_counts, pair_count, points, weights, pair_slot))


def main_kernel(
    train_counts_hbm, received_ref, packed_weights_ref, packed_points_ref, packed_times_ref,
    partial_ref,
    rows_ref, sums_ref, block_slot, slot_row, train_counts_ref, sem,
):
    fetch = pltpu.make_async_copy(train_counts_hbm, train_counts_ref, sem)
    fetch.start()
    slots, test_tile, columns = partial_ref.shape
    senders = received_ref.shape[0] // slots
    own_tiles = train_counts_ref.shape[0] // senders
    depth = packed_points_ref.shape[0]
    row8 = lax.broadcasted_iota(i32, (8, test_tile), 0)
    per_slot = test_tile // BLOCK
    sums_ref[...] = jnp.zeros(sums_ref.shape, f32)
    together = math.gcd(slots, 16)

    def place(step, offset):
        operands, counts = [], []
        for i in range(together):
            g = step * together + i
            got = received_ref[g * senders]
            for s in range(1, senders):
                got = got + received_ref[g * senders + s]
            counts.append(jnp.max(got[3:4, :]).astype(i32))
            v = SCALE * (jnp.concatenate([got, got], axis=0) - 1.0)
            square = jnp.sum(jnp.where(row8 < 3, v * v, 0.0), axis=0, keepdims=True)
            raw = jnp.where(
                row8 < 3, -2.0 * v, jnp.where(row8 == 3, 1.0, jnp.where(row8 == 4, square, 0.0))
            )
            high, mid, low = split3(raw)
            operand = jnp.concatenate([high, high, mid, mid, high, low], axis=0).T
            lanes = jnp.zeros((test_tile, rows_ref.shape[1] - depth), f32)
            operands.append(jnp.concatenate([operand, lanes], axis=1).astype(bf16))
        for i in range(together):
            g = step * together + i
            start = pl.multiple_of(offset * BLOCK, BLOCK)
            rows_ref[pl.ds(start, test_tile), :] = operands[i]
            slot_row[g] = offset
            for b in range(per_slot):
                block_slot[offset + b] = g
            offset = offset + (counts[i] + BLOCK - 1) // BLOCK
        return offset

    blocks = lax.fori_loop(0, slots // together, place, jnp.int32(0))
    fetch.wait()
    first_tile = lax.axis_index("narrow") * own_tiles
    total = lax.fori_loop(
        0, own_tiles, lambda t, a: a + train_counts_ref[first_tile + t], jnp.int32(0)
    )
    for b in range(2 * PART):
        block_slot[blocks + b] = 0
    parts = (blocks + PART - 1) // PART
    parts = jnp.where(parts < 3, 3, jnp.where(parts == 5, 6, parts))
    steps = (parts + PARTS - 1) // PARTS
    shorter = PARTS * steps - parts
    longer = steps - shorter
    col_tiles = (total + COLS - 1) // COLS
    nothing = jnp.zeros((BLOCK, DEPTH), bf16)
    ring = PARTS * PART

    def with_accumulators(*accs):
        square_accs, sum_accs = accs[: ring + 1], accs[ring + 1 :]
        for acc in accs:
            pltpu.matmul_pop(acc)

        def push_points(c):
            rows = packed_points_ref[:, pl.ds(pl.multiple_of(c * COLS, COLS), COLS)]
            pltpu.matmul_push_rhs(
                jnp.concatenate([rows, jnp.zeros((DEPTH - depth, COLS), bf16)], axis=0), 0, 0
            )

        def take_points():
            pltpu.matmul_acc_lhs(square_accs[ring], nothing, load_staged_rhs=0)

        def push_weights(c):
            rows = packed_weights_ref[pl.ds(pl.multiple_of(c * COLS, COLS), COLS), :]
            pltpu.matmul_push_rhs(
                jnp.concatenate([rows, jnp.zeros((COLS, DEPTH - columns), bf16)], axis=1), 0, 1
            )

        def take_weights():
            pltpu.matmul_acc_lhs(sum_accs[ring], nothing, load_staged_rhs=0)

        def block_rows(part, b):
            return pl.ds(pl.multiple_of(part * (PART * BLOCK) + b * BLOCK, BLOCK), BLOCK)

        def start_squares(part, b):
            rows = rows_ref[block_rows(part, b), :]
            pltpu.matmul_acc_lhs(
                square_accs[b],
                jnp.concatenate([rows, jnp.zeros((BLOCK, DEPTH - rows.shape[1]), bf16)], axis=1),
            )

        def gather_sums(part, b):
            rows = block_rows(part, b)
            sums_ref[rows, :] = sums_ref[rows, :] + pltpu.matmul_pop(sum_accs[b])[:, :columns]

        def evaluate(c, part, count, after, before):
            col = pl.ds(pl.multiple_of(c * COLS, COLS), COLS)
            for b in range(ring):
                square = pltpu.matmul_pop(square_accs[b])
                start_squares(after, b)
                gather_sums(before, b)
                if b < count * PART:
                    square = jnp.maximum(square, 1e-30)
                    times = packed_times_ref[pl.ds(block_slot[part * PART + b], 1), col]
                    falloff = jnp.maximum(SCALE - square * lax.rsqrt(square), 0.0)
                    second = falloff * falloff
                    kernel = (second * second * (1.25 * SCALE - falloff) * times).astype(bf16)
                    pltpu.matmul_acc_lhs(sum_accs[b], kernel)

        def last_step(c, before, count):
            take_points()
            push_weights(c + 1)
            evaluate(c, parts - count, count, 0, before)
            take_weights()
            push_points(jnp.minimum(c + 2, col_tiles))

        def col_step(c, before):
            def long_step(q, before):
                part = PARTS * q
                evaluate(c, part, PARTS, part + PARTS, before)
                return part

            def short_step(q, before):
                part = PARTS * longer + (PARTS - 1) * q
                evaluate(c, part, PARTS - 1, part + (PARTS - 1), before)
                return part

            before = lax.fori_loop(0, longer - (shorter == 0).astype(i32), long_step, before)
            before = lax.fori_loop(0, shorter - 1, short_step, before)
            pl.when(shorter == 0)(functools.partial(last_step, c, before, PARTS))
            pl.when(shorter > 0)(functools.partial(last_step, c, before, PARTS - 1))
            return parts - jnp.where(shorter == 0, PARTS, PARTS - 1)

        push_points(jnp.int32(0))
        take_points()
        push_points(jnp.int32(1))
        push_weights(jnp.int32(0))
        take_weights()
        for b in range(ring):
            start_squares(jnp.int32(0), b)
        before = lax.fori_loop(0, col_tiles, col_step, jnp.int32(0))
        for b in range(ring):
            gather_sums(before, b)
            pltpu.matmul_pop(square_accs[b])
        take_points()
        pltpu.matmul_pop(square_accs[ring])
        pltpu.matmul_pop(sum_accs[ring])

    pl.run_scoped(
        with_accumulators,
        *[pltpu.ACC(mxu)((BLOCK, DEPTH), f32) for mxu in range(2) for _ in range(ring + 1)],
    )

    def give(step, carry):
        for i in range(together):
            g = step * together + i
            start = pl.multiple_of(slot_row[g] * BLOCK, BLOCK)
            partial_ref[g] = sums_ref[pl.ds(start, test_tile), :].astype(bf16)
        return carry

    lax.fori_loop(0, slots // together, give, 0)


def partials(train_counts, received, packed, slots, columns):
    test_tile = received.shape[2]
    step_rows = PARTS * PART * BLOCK
    height = max(slots * test_tile, 6 * PART * BLOCK) + step_rows
    return pl.pallas_call(
        main_kernel,
        out_shape=jax.ShapeDtypeStruct((slots, test_tile, columns), bf16),
        in_specs=[HBM, VMEM, VMEM, VMEM, VMEM],
        out_specs=VMEM,
        scratch_shapes=[
            pltpu.VMEM((height, 128), bf16),
            pltpu.VMEM((height, columns), f32),
            pltpu.SMEM((height // BLOCK,), i32),
            pltpu.SMEM((slots,), i32),
            pltpu.SMEM(train_counts.shape, i32),
            pltpu.SemaphoreType.DMA(()),
        ],
        compiler_params=pltpu.CompilerParams(vmem_limit_bytes=VMEM_LIMIT),
        cost_estimate=pl.CostEstimate(flops=3_000_000_000, bytes_accessed=4_000_000, transcendentals=8_000_000),
        name="partials",
    )(*stay(train_counts), received, *packed)


def collect_kernel(shift, slot_tile_ref, collected_ref, out_ref):
    sources = collected_ref.shape[0]
    tiles = out_ref.shape[0]
    group = lax.axis_index("wide")
    first = lax.rem(lax.axis_index("narrow") + shift, lax.axis_size("narrow")) * tiles
    acc = [jnp.zeros(out_ref.shape[1:], f32) for _ in range(tiles)]
    for w in range(sources):
        block = collected_ref[w].astype(f32)
        tile = slot_tile_ref[w, group] - first
        for t in range(tiles):
            acc[t] = acc[t] + jnp.where(tile == t, block, 0.0)
    for t in range(tiles):
        out_ref[t] = acc[t].astype(out_ref.dtype)


def collect(shift, slot_tile, collected, tiles, dtype):
    return pl.pallas_call(
        functools.partial(collect_kernel, shift),
        out_shape=jax.ShapeDtypeStruct((tiles,) + collected.shape[1:], dtype),
        in_specs=[SMEM, VMEM],
        out_specs=VMEM,
        compiler_params=pltpu.CompilerParams(vmem_limit_bytes=VMEM_LIMIT),
        cost_estimate=pl.CostEstimate(flops=1_000_000, bytes_accessed=700_000, transcendentals=0),
        name="collect",
    )(slot_tile, collected)


def body(
    train_points, train_weights, train_counts, test_points, prior, test_counts, pair_count, pair_slot, slot_tile
):
    narrow_size = lax.axis_size("narrow")
    own_tests = test_points.shape[0]
    slots = slot_tile.shape[0]
    columns = train_weights.shape[2]
    offered = offer(slot_tile, test_counts, jnp.transpose(test_points, (1, 0, 2)), slots * narrow_size)
    received = lax.all_to_all(offered, ("wide", "narrow"), 0, 0, tiled=True)
    packed = prepare(
        train_counts, pair_count, jnp.transpose(train_points, (1, 0, 2)), train_weights, pair_slot, slots
    )
    partial_value = partials(train_counts, received, packed, slots, columns)
    collected = lax.all_to_all(partial_value, "wide", 0, 0, tiled=True)
    arrived = []
    for k in range(1, narrow_size):
        sent = collect(k, slot_tile, collected, own_tests, bf16)
        arrived.append(
            lax.ppermute(sent, "narrow", [(i, (i + k) % narrow_size) for i in range(narrow_size)])
        )
    owned = collect(0, slot_tile, collected, own_tests, f32)
    for part in arrived:
        owned = owned + part.astype(f32)
    test_live = jnp.arange(prior.shape[1], dtype=i32)[None, :] < test_counts[:, None]
    update = jnp.where(test_live[:, :, None], owned, 0.0)
    return (prior.astype(f32) + update).astype(bf16)


def solution(mesh):
    return jax.shard_map(
        body,
        mesh=mesh,
        in_specs=(
            P("wide", None, None),
            P(("wide", "narrow"), None, None),
            P("wide"),
            P(("wide", "narrow"), None, None),
            P(("wide", "narrow"), None, None),
            P(("wide", "narrow")),
            P("wide"),
            P("wide", None),
            P(),
        ),
        out_specs=P(("wide", "narrow"), None, None),
        check_vma=False,
    )
```

```python
import functools
import math

import jax
import jax.numpy as jnp
from jax import lax
from jax.experimental import pallas as pl
from jax.experimental.pallas import tpu as pltpu
from jax.sharding import PartitionSpec as P

f32, bf16, i32 = jnp.float32, jnp.bfloat16, jnp.int32
COLS = 256
BLOCK = 16
PART = 8
PARTS = 4
DEPTH = 256
SCALE = 4.0**0.2
VMEM_LIMIT = 32 * 1024 * 1024
VMEM = pl.BlockSpec(memory_space=pltpu.VMEM)
SMEM = pl.BlockSpec(memory_space=pltpu.SMEM)
HBM = pl.BlockSpec(memory_space=pltpu.HBM)


def split3(x):
    high = x.astype(bf16).astype(f32)
    rest = x - high
    mid = rest.astype(bf16).astype(f32)
    low = (rest - mid).astype(bf16).astype(f32)
    return high, mid, low


def stay(*arrays):
    return [pltpu.with_memory_space_constraint(array, pltpu.HBM) for array in arrays]


def offer_kernel(slot_tile_hbm, test_counts_hbm, test_points_hbm, offer_ref, slot_tile, test_counts, points, sems):
    axes, own_tests, test_tile = points.shape
    senders = offer_ref.shape[0]
    wide_size = slot_tile.shape[0]
    copies = [
        pltpu.make_async_copy(source, target, sems.at[i])
        for i, (source, target) in enumerate(
            ((slot_tile_hbm, slot_tile), (test_counts_hbm, test_counts), (test_points_hbm, points))
        )
    ]
    for copy in copies:
        copy.start()
    first = lax.axis_index("narrow") * own_tests
    group = lax.axis_index("wide")
    for copy in copies:
        copy.wait()
    payloads = [
        jnp.concatenate(
            [
                *(points[axis, t : t + 1, :] for axis in range(axes)),
                jnp.full((1, test_tile), test_counts[t].astype(f32), f32),
            ],
            axis=0,
        )
        for t in range(own_tests)
    ]
    narrow_size = senders // wide_size

    def step(w, carry):
        wanted = slot_tile[w, group] - first
        chosen = jnp.zeros((axes + 1, test_tile), f32)
        for t in range(own_tests):
            chosen = jnp.where(wanted == t, payloads[t], chosen)
        for n in range(narrow_size):
            offer_ref[w * narrow_size + n] = chosen
        return carry

    lax.fori_loop(0, wide_size, step, 0, unroll=4)


def offer(slot_tile, test_counts, test_points, senders):
    axes, own_tests, test_tile = test_points.shape
    return pl.pallas_call(
        offer_kernel,
        out_shape=jax.ShapeDtypeStruct((senders, axes + 1, test_tile), f32),
        in_specs=[HBM, HBM, HBM],
        out_specs=VMEM,
        scratch_shapes=[
            pltpu.SMEM(slot_tile.shape, i32),
            pltpu.SMEM(test_counts.shape, i32),
            pltpu.VMEM(test_points.shape, f32),
            pltpu.SemaphoreType.DMA((3,)),
        ],
        compiler_params=pltpu.CompilerParams(vmem_limit_bytes=VMEM_LIMIT),
        cost_estimate=pl.CostEstimate(flops=100_000, bytes_accessed=100_000, transcendentals=0),
        name="offer",
    )(*stay(slot_tile, test_counts, test_points))


def prepare_kernel(
    train_counts_hbm, pair_count_hbm, points_hbm, weights_hbm, pair_slot_hbm,
    packed_weights_ref, packed_points_ref, packed_times_ref,
    wide_weights, raw_points, train_counts_ref, pair_count_ref, points_ref, weights_ref, pair_slot_ref, sems,
):
    own_tiles, tile, columns = weights_ref.shape
    copies = [
        pltpu.make_async_copy(source, target, sems.at[i])
        for i, (source, target) in enumerate(
            (
                (train_counts_hbm, train_counts_ref),
                (pair_count_hbm, pair_count_ref),
                (points_hbm, points_ref),
                (weights_hbm, weights_ref),
                (pair_slot_hbm, pair_slot_ref),
            )
        )
    ]
    for copy in copies:
        copy.start()
    for copy in copies:
        copy.wait()
    slots = packed_times_ref.shape[0]
    list_length = pair_slot_ref.shape[1]
    first_tile = lax.axis_index("narrow") * own_tiles
    window = tile + 128
    positions = lax.broadcasted_iota(i32, (1, list_length), 1)
    named = pair_slot_ref[...]
    one_hot = (
        lax.broadcasted_iota(i32, (slots, list_length), 0) == jnp.broadcast_to(named, (slots, list_length))
    ).astype(f32)
    row8 = lax.broadcasted_iota(i32, (8, tile), 0)
    lane = lax.broadcasted_iota(i32, (8, window), 1)
    lane_slots = lax.broadcasted_iota(i32, (slots, window), 1)

    def skip(t, total):
        return total + pair_count_ref[t]

    first_pair = lax.fori_loop(0, first_tile, skip, jnp.int32(0))

    def step(t, carry):
        offset, pair = carry
        u = [
            SCALE * (points_ref[axis, pl.ds(first_tile + t, 1), :] - 1.0)
            for axis in range(points_ref.shape[0])
        ]
        square = u[0] * u[0] + u[1] * u[1] + u[2] * u[2]
        raw = jnp.where(row8 == 4, 1.0, 0.0)
        for row, value in enumerate((*u, square)):
            raw = jnp.where(row8 == row, value, raw)
        pair_end = pair + pair_count_ref[first_tile + t]
        inside = jnp.logical_and(positions >= pair, positions < pair_end)
        times = jnp.sum(jnp.where(inside, one_hot, 0.0), axis=1, keepdims=True)
        shift = lax.rem(offset, 128)
        base = pl.multiple_of(offset - shift, 128)
        rolled = pltpu.roll(
            jnp.concatenate([raw, jnp.zeros((8, 128), f32)], axis=1), shift, 1
        )
        spot = pl.ds(base, window)
        raw_points[:, spot] = jnp.where(lane >= shift, rolled, raw_points[:, spot])
        packed_times_ref[:, spot] = jnp.where(
            lane_slots >= shift, times, packed_times_ref[:, spot]
        )
        wide_weights[pl.ds(offset, tile), :] = weights_ref[t].astype(f32)
        return offset + train_counts_ref[first_tile + t], pair_end

    total, _ = lax.fori_loop(0, own_tiles, step, (jnp.int32(0), first_pair))
    shift = lax.rem(total, 128)
    base = pl.multiple_of(total - shift, 128)
    tail = COLS + 128
    spot = pl.ds(base, tail)
    raw_points[:, spot] = jnp.where(
        lax.broadcasted_iota(i32, (8, tail), 1) >= shift, 0.0, raw_points[:, spot]
    )
    packed_times_ref[:, spot] = jnp.where(
        lax.broadcasted_iota(i32, (slots, tail), 1) >= shift, 0.0, packed_times_ref[:, spot]
    )
    wide_weights[pl.ds(total, COLS), :] = jnp.zeros((COLS, columns), f32)

    def finish(c, carry):
        start = pl.multiple_of(c * COLS, COLS)
        high, mid, low = split3(raw_points[:, pl.ds(start, COLS)])
        packed_points_ref[:, pl.ds(start, COLS)] = jnp.concatenate(
            [high, mid, high, mid, low, high], axis=0
        ).astype(bf16)
        packed_weights_ref[pl.ds(start, COLS), :] = wide_weights[pl.ds(start, COLS), :].astype(bf16)
        return carry

    lax.fori_loop(0, (total + COLS - 1) // COLS, finish, 0)


def prepare(train_counts, pair_count, points, weights, pair_slot, slots):
    own_tiles, tile, columns = weights.shape
    length = own_tiles * tile + COLS + 128
    return pl.pallas_call(
        prepare_kernel,
        out_shape=(
            jax.ShapeDtypeStruct((length, columns), bf16),
            jax.ShapeDtypeStruct((48, length), bf16),
            jax.ShapeDtypeStruct((slots, length), f32),
        ),
        in_specs=[HBM] * 5,
        out_specs=(VMEM, VMEM, VMEM),
        scratch_shapes=[
            pltpu.VMEM((length, columns), f32),
            pltpu.VMEM((8, length), f32),
            pltpu.SMEM(train_counts.shape, i32),
            pltpu.SMEM(pair_count.shape, i32),
            pltpu.VMEM(points.shape, f32),
            pltpu.VMEM(weights.shape, bf16),
            pltpu.VMEM(pair_slot.shape, i32),
            pltpu.SemaphoreType.DMA((5,)),
        ],
        compiler_params=pltpu.CompilerParams(vmem_limit_bytes=VMEM_LIMIT),
        cost_estimate=pl.CostEstimate(flops=40_000_000, bytes_accessed=4_000_000, transcendentals=0),
        name="prepare",
    )(*stay(train_counts, pair_count, points, weights, pair_slot))


def main_kernel(
    train_counts_hbm, received_ref, packed_weights_ref, packed_points_ref, packed_times_ref,
    partial_ref,
    rows_ref, sums_ref, block_slot, slot_row, train_counts_ref, sem,
):
    fetch = pltpu.make_async_copy(train_counts_hbm, train_counts_ref, sem)
    fetch.start()
    slots, test_tile, columns = partial_ref.shape
    senders = received_ref.shape[0] // slots
    own_tiles = train_counts_ref.shape[0] // senders
    depth = packed_points_ref.shape[0]
    row8 = lax.broadcasted_iota(i32, (8, test_tile), 0)
    per_slot = test_tile // BLOCK
    sums_ref[...] = jnp.zeros(sums_ref.shape, f32)
    together = math.gcd(slots, 16)

    def place(step, offset):
        operands, counts = [], []
        for i in range(together):
            g = step * together + i
            got = received_ref[g * senders]
            for s in range(1, senders):
                got = got + received_ref[g * senders + s]
            counts.append(jnp.max(got[3:4, :]).astype(i32))
            v = SCALE * (jnp.concatenate([got, got], axis=0) - 1.0)
            square = jnp.sum(jnp.where(row8 < 3, v * v, 0.0), axis=0, keepdims=True)
            raw = jnp.where(
                row8 < 3, -2.0 * v, jnp.where(row8 == 3, 1.0, jnp.where(row8 == 4, square, 0.0))
            )
            high, mid, low = split3(raw)
            operand = jnp.concatenate([high, high, mid, mid, high, low], axis=0).T
            lanes = jnp.zeros((test_tile, rows_ref.shape[1] - depth), f32)
            operands.append(jnp.concatenate([operand, lanes], axis=1).astype(bf16))
        for i in range(together):
            g = step * together + i
            start = pl.multiple_of(offset * BLOCK, BLOCK)
            rows_ref[pl.ds(start, test_tile), :] = operands[i]
            slot_row[g] = offset
            for b in range(per_slot):
                block_slot[offset + b] = g
            offset = offset + (counts[i] + BLOCK - 1) // BLOCK
        return offset

    blocks = lax.fori_loop(0, slots // together, place, jnp.int32(0))
    fetch.wait()
    first_tile = lax.axis_index("narrow") * own_tiles
    total = lax.fori_loop(
        0, own_tiles, lambda t, a: a + train_counts_ref[first_tile + t], jnp.int32(0)
    )
    for b in range(2 * PART):
        block_slot[blocks + b] = 0
    parts = (blocks + PART - 1) // PART
    parts = jnp.where(parts < 3, 3, jnp.where(parts == 5, 6, parts))
    steps = (parts + PARTS - 1) // PARTS
    shorter = PARTS * steps - parts
    longer = steps - shorter
    col_tiles = (total + COLS - 1) // COLS
    nothing = jnp.zeros((BLOCK, DEPTH), bf16)
    ring = PARTS * PART

    def with_accumulators(*accs):
        square_accs, sum_accs = accs[: ring + 1], accs[ring + 1 :]
        for acc in accs:
            pltpu.matmul_pop(acc)

        def push_points(c):
            rows = packed_points_ref[:, pl.ds(pl.multiple_of(c * COLS, COLS), COLS)]
            pltpu.matmul_push_rhs(
                jnp.concatenate([rows, jnp.zeros((DEPTH - depth, COLS), bf16)], axis=0), 0, 0
            )

        def take_points():
            pltpu.matmul_acc_lhs(square_accs[ring], nothing, load_staged_rhs=0)

        def push_weights(c):
            rows = packed_weights_ref[pl.ds(pl.multiple_of(c * COLS, COLS), COLS), :]
            pltpu.matmul_push_rhs(
                jnp.concatenate([rows, jnp.zeros((COLS, DEPTH - columns), bf16)], axis=1), 0, 1
            )

        def take_weights():
            pltpu.matmul_acc_lhs(sum_accs[ring], nothing, load_staged_rhs=0)

        def block_rows(part, b):
            return pl.ds(pl.multiple_of(part * (PART * BLOCK) + b * BLOCK, BLOCK), BLOCK)

        def start_squares(part, b):
            rows = rows_ref[block_rows(part, b), :]
            pltpu.matmul_acc_lhs(
                square_accs[b],
                jnp.concatenate([rows, jnp.zeros((BLOCK, DEPTH - rows.shape[1]), bf16)], axis=1),
            )

        def gather_sums(part, b):
            rows = block_rows(part, b)
            sums_ref[rows, :] = sums_ref[rows, :] + pltpu.matmul_pop(sum_accs[b])[:, :columns]

        def evaluate(c, part, count, after, before):
            col = pl.ds(pl.multiple_of(c * COLS, COLS), COLS)
            for b in range(ring):
                square = pltpu.matmul_pop(square_accs[b])
                start_squares(after, b)
                gather_sums(before, b)
                if b < count * PART:
                    square = jnp.maximum(square, 1e-30)
                    times = packed_times_ref[pl.ds(block_slot[part * PART + b], 1), col]
                    falloff = jnp.maximum(SCALE - square * lax.rsqrt(square), 0.0)
                    second = falloff * falloff
                    kernel = (second * second * (1.25 * SCALE - falloff) * times).astype(bf16)
                    pltpu.matmul_acc_lhs(sum_accs[b], kernel)

        def last_step(c, before, count):
            take_points()
            push_weights(c + 1)
            evaluate(c, parts - count, count, 0, before)
            take_weights()
            push_points(jnp.minimum(c + 2, col_tiles))

        def col_step(c, before):
            def long_step(q, before):
                part = PARTS * q
                evaluate(c, part, PARTS, part + PARTS, before)
                return part

            def short_step(q, before):
                part = PARTS * longer + (PARTS - 1) * q
                evaluate(c, part, PARTS - 1, part + (PARTS - 1), before)
                return part

            before = lax.fori_loop(0, longer - (shorter == 0).astype(i32), long_step, before)
            before = lax.fori_loop(0, shorter - 1, short_step, before)
            pl.when(shorter == 0)(functools.partial(last_step, c, before, PARTS))
            pl.when(shorter > 0)(functools.partial(last_step, c, before, PARTS - 1))
            return parts - jnp.where(shorter == 0, PARTS, PARTS - 1)

        push_points(jnp.int32(0))
        take_points()
        push_points(jnp.int32(1))
        push_weights(jnp.int32(0))
        take_weights()
        for b in range(ring):
            start_squares(jnp.int32(0), b)
        before = lax.fori_loop(0, col_tiles, col_step, jnp.int32(0))
        for b in range(ring):
            gather_sums(before, b)
            pltpu.matmul_pop(square_accs[b])
        take_points()
        pltpu.matmul_pop(square_accs[ring])
        pltpu.matmul_pop(sum_accs[ring])

    pl.run_scoped(
        with_accumulators,
        *[pltpu.ACC(mxu)((BLOCK, DEPTH), f32) for mxu in range(2) for _ in range(ring + 1)],
    )

    def give(step, carry):
        for i in range(together):
            g = step * together + i
            start = pl.multiple_of(slot_row[g] * BLOCK, BLOCK)
            partial_ref[g] = sums_ref[pl.ds(start, test_tile), :].astype(bf16)
        return carry

    lax.fori_loop(0, slots // together, give, 0)


def partials(train_counts, received, packed, slots, columns):
    test_tile = received.shape[2]
    step_rows = PARTS * PART * BLOCK
    height = max(slots * test_tile, 6 * PART * BLOCK) + step_rows
    return pl.pallas_call(
        main_kernel,
        out_shape=jax.ShapeDtypeStruct((slots, test_tile, columns), bf16),
        in_specs=[HBM, VMEM, VMEM, VMEM, VMEM],
        out_specs=VMEM,
        scratch_shapes=[
            pltpu.VMEM((height, 128), bf16),
            pltpu.VMEM((height, columns), f32),
            pltpu.SMEM((height // BLOCK,), i32),
            pltpu.SMEM((slots,), i32),
            pltpu.SMEM(train_counts.shape, i32),
            pltpu.SemaphoreType.DMA(()),
        ],
        compiler_params=pltpu.CompilerParams(vmem_limit_bytes=VMEM_LIMIT),
        cost_estimate=pl.CostEstimate(flops=3_000_000_000, bytes_accessed=4_000_000, transcendentals=8_000_000),
        name="partials",
    )(*stay(train_counts), received, *packed)


def collect_kernel(shift, slot_tile_ref, collected_ref, out_ref, sums_ref):
    sources = collected_ref.shape[0]
    tiles = out_ref.shape[0]
    group = lax.axis_index("wide")
    first = lax.rem(lax.axis_index("narrow") + shift, lax.axis_size("narrow")) * tiles
    sums_ref[...] = jnp.zeros(sums_ref.shape, f32)
    for w in range(sources):
        tile = slot_tile_ref[w, group] - first
        spot = jnp.where(jnp.logical_and(tile >= 0, tile < tiles), tile, tiles)
        sums_ref[spot] = sums_ref[spot] + collected_ref[w].astype(f32)
    for t in range(tiles):
        out_ref[t] = sums_ref[t].astype(out_ref.dtype)


def collect(shift, slot_tile, collected, tiles, dtype):
    return pl.pallas_call(
        functools.partial(collect_kernel, shift),
        out_shape=jax.ShapeDtypeStruct((tiles,) + collected.shape[1:], dtype),
        in_specs=[SMEM, VMEM],
        out_specs=VMEM,
        scratch_shapes=[pltpu.VMEM((tiles + 1,) + collected.shape[1:], f32)],
        compiler_params=pltpu.CompilerParams(vmem_limit_bytes=VMEM_LIMIT),
        cost_estimate=pl.CostEstimate(flops=1_000_000, bytes_accessed=700_000, transcendentals=0),
        name="collect",
    )(slot_tile, collected)


def body(
    train_points, train_weights, train_counts, test_points, prior, test_counts, pair_count, pair_slot, slot_tile
):
    narrow_size = lax.axis_size("narrow")
    own_tests = test_points.shape[0]
    slots = slot_tile.shape[0]
    columns = train_weights.shape[2]
    offered = offer(slot_tile, test_counts, jnp.transpose(test_points, (1, 0, 2)), slots * narrow_size)
    received = lax.all_to_all(offered, ("wide", "narrow"), 0, 0, tiled=True)
    packed = prepare(
        train_counts, pair_count, jnp.transpose(train_points, (1, 0, 2)), train_weights, pair_slot, slots
    )
    partial_value = partials(train_counts, received, packed, slots, columns)
    collected = lax.all_to_all(partial_value, "wide", 0, 0, tiled=True)
    arrived = []
    for k in range(1, narrow_size):
        sent = collect(k, slot_tile, collected, own_tests, bf16)
        arrived.append(
            lax.ppermute(sent, "narrow", [(i, (i + k) % narrow_size) for i in range(narrow_size)])
        )
    owned = collect(0, slot_tile, collected, own_tests, f32)
    for part in arrived:
        owned = owned + part.astype(f32)
    test_live = jnp.arange(prior.shape[1], dtype=i32)[None, :] < test_counts[:, None]
    update = jnp.where(test_live[:, :, None], owned, 0.0)
    return (prior.astype(f32) + update).astype(bf16)


def solution(mesh):
    return jax.shard_map(
        body,
        mesh=mesh,
        in_specs=(
            P("wide", None, None),
            P(("wide", "narrow"), None, None),
            P("wide"),
            P(("wide", "narrow"), None, None),
            P(("wide", "narrow"), None, None),
            P(("wide", "narrow")),
            P("wide"),
            P("wide", None),
            P(),
        ),
        out_specs=P(("wide", "narrow"), None, None),
        check_vma=False,
    )
```

```python
import functools
import math

import jax
import jax.numpy as jnp
from jax import lax
from jax.experimental import pallas as pl
from jax.experimental.pallas import tpu as pltpu
from jax.sharding import PartitionSpec as P

f32, bf16, i32 = jnp.float32, jnp.bfloat16, jnp.int32
COLS = 256
BLOCK = 16
PART = 8
PARTS = 4
DEPTH = 256
SCALE = 4.0**0.2
VMEM_LIMIT = 32 * 1024 * 1024
VMEM = pl.BlockSpec(memory_space=pltpu.VMEM)
SMEM = pl.BlockSpec(memory_space=pltpu.SMEM)
HBM = pl.BlockSpec(memory_space=pltpu.HBM)


def split3(x):
    high = x.astype(bf16).astype(f32)
    rest = x - high
    mid = rest.astype(bf16).astype(f32)
    low = (rest - mid).astype(bf16).astype(f32)
    return high, mid, low


def stay(*arrays):
    return [pltpu.with_memory_space_constraint(array, pltpu.HBM) for array in arrays]


def offer_kernel(slot_tile_hbm, test_counts_hbm, test_points_hbm, offer_ref, slot_tile, test_counts, points, sems):
    axes, own_tests, test_tile = points.shape
    senders = offer_ref.shape[0]
    wide_size = slot_tile.shape[0]
    copies = [
        pltpu.make_async_copy(source, target, sems.at[i])
        for i, (source, target) in enumerate(
            ((slot_tile_hbm, slot_tile), (test_counts_hbm, test_counts), (test_points_hbm, points))
        )
    ]
    for copy in copies:
        copy.start()
    first = lax.axis_index("narrow") * own_tests
    group = lax.axis_index("wide")
    for copy in copies:
        copy.wait()
    payloads = [
        jnp.concatenate(
            [
                *(points[axis, t : t + 1, :] for axis in range(axes)),
                jnp.full((1, test_tile), test_counts[t].astype(f32), f32),
            ],
            axis=0,
        )
        for t in range(own_tests)
    ]
    narrow_size = senders // wide_size

    def step(w, carry):
        wanted = slot_tile[w, group] - first
        chosen = jnp.zeros((axes + 1, test_tile), f32)
        for t in range(own_tests):
            chosen = jnp.where(wanted == t, payloads[t], chosen)
        for n in range(narrow_size):
            offer_ref[w * narrow_size + n] = chosen
        return carry

    lax.fori_loop(0, wide_size, step, 0, unroll=4)


def offer(slot_tile, test_counts, test_points, senders):
    axes, own_tests, test_tile = test_points.shape
    return pl.pallas_call(
        offer_kernel,
        out_shape=jax.ShapeDtypeStruct((senders, axes + 1, test_tile), f32),
        in_specs=[HBM, HBM, HBM],
        out_specs=VMEM,
        scratch_shapes=[
            pltpu.SMEM(slot_tile.shape, i32),
            pltpu.SMEM(test_counts.shape, i32),
            pltpu.VMEM(test_points.shape, f32),
            pltpu.SemaphoreType.DMA((3,)),
        ],
        compiler_params=pltpu.CompilerParams(vmem_limit_bytes=VMEM_LIMIT),
        cost_estimate=pl.CostEstimate(flops=100_000, bytes_accessed=100_000, transcendentals=0),
        name="offer",
    )(*stay(slot_tile, test_counts, test_points))


def prepare_kernel(
    train_counts_hbm, pair_count_hbm, points_hbm, weights_hbm, pair_slot_hbm,
    packed_weights_ref, packed_points_ref, packed_times_ref,
    wide_weights, raw_points, train_counts_ref, pair_count_ref, points_ref, weights_ref, pair_slot_ref, sems,
):
    own_tiles, tile, columns = weights_ref.shape
    copies = [
        pltpu.make_async_copy(source, target, sems.at[i])
        for i, (source, target) in enumerate(
            (
                (train_counts_hbm, train_counts_ref),
                (pair_count_hbm, pair_count_ref),
                (points_hbm, points_ref),
                (weights_hbm, weights_ref),
                (pair_slot_hbm, pair_slot_ref),
            )
        )
    ]
    for copy in copies:
        copy.start()
    for copy in copies:
        copy.wait()
    slots = packed_times_ref.shape[0]
    list_length = pair_slot_ref.shape[1]
    first_tile = lax.axis_index("narrow") * own_tiles
    window = tile + 128
    positions = lax.broadcasted_iota(i32, (1, list_length), 1)
    named = pair_slot_ref[...]
    one_hot = (
        lax.broadcasted_iota(i32, (slots, list_length), 0) == jnp.broadcast_to(named, (slots, list_length))
    ).astype(f32)
    row8 = lax.broadcasted_iota(i32, (8, tile), 0)
    lane = lax.broadcasted_iota(i32, (8, window), 1)
    lane_slots = lax.broadcasted_iota(i32, (slots, window), 1)

    def skip(t, total):
        return total + pair_count_ref[t]

    first_pair = lax.fori_loop(0, first_tile, skip, jnp.int32(0))

    def step(t, carry):
        offset, pair = carry
        u = [
            SCALE * (points_ref[axis, pl.ds(first_tile + t, 1), :] - 1.0)
            for axis in range(points_ref.shape[0])
        ]
        square = u[0] * u[0] + u[1] * u[1] + u[2] * u[2]
        raw = jnp.where(row8 == 4, 1.0, 0.0)
        for row, value in enumerate((*u, square)):
            raw = jnp.where(row8 == row, value, raw)
        pair_end = pair + pair_count_ref[first_tile + t]
        inside = jnp.logical_and(positions >= pair, positions < pair_end)
        times = jnp.sum(jnp.where(inside, one_hot, 0.0), axis=1, keepdims=True)
        shift = lax.rem(offset, 128)
        base = pl.multiple_of(offset - shift, 128)
        rolled = pltpu.roll(
            jnp.concatenate([raw, jnp.zeros((8, 128), f32)], axis=1), shift, 1
        )
        spot = pl.ds(base, window)
        raw_points[:, spot] = jnp.where(lane >= shift, rolled, raw_points[:, spot])
        packed_times_ref[:, spot] = jnp.where(
            lane_slots >= shift, times, packed_times_ref[:, spot]
        )
        wide_weights[pl.ds(offset, tile), :] = weights_ref[t].astype(f32)
        return offset + train_counts_ref[first_tile + t], pair_end

    total, _ = lax.fori_loop(0, own_tiles, step, (jnp.int32(0), first_pair))
    shift = lax.rem(total, 128)
    base = pl.multiple_of(total - shift, 128)
    tail = COLS + 128
    spot = pl.ds(base, tail)
    raw_points[:, spot] = jnp.where(
        lax.broadcasted_iota(i32, (8, tail), 1) >= shift, 0.0, raw_points[:, spot]
    )
    packed_times_ref[:, spot] = jnp.where(
        lax.broadcasted_iota(i32, (slots, tail), 1) >= shift, 0.0, packed_times_ref[:, spot]
    )
    wide_weights[pl.ds(total, COLS), :] = jnp.zeros((COLS, columns), f32)

    def finish(c, carry):
        start = pl.multiple_of(c * COLS, COLS)
        high, mid, low = split3(raw_points[:, pl.ds(start, COLS)])
        packed_points_ref[:, pl.ds(start, COLS)] = jnp.concatenate(
            [high, mid, high, mid, low, high], axis=0
        ).astype(bf16)
        packed_weights_ref[pl.ds(start, COLS), :] = wide_weights[pl.ds(start, COLS), :].astype(bf16)
        return carry

    lax.fori_loop(0, (total + COLS - 1) // COLS, finish, 0)


def prepare(train_counts, pair_count, points, weights, pair_slot, slots):
    own_tiles, tile, columns = weights.shape
    length = own_tiles * tile + COLS + 128
    return pl.pallas_call(
        prepare_kernel,
        out_shape=(
            jax.ShapeDtypeStruct((length, columns), bf16),
            jax.ShapeDtypeStruct((48, length), bf16),
            jax.ShapeDtypeStruct((slots, length), f32),
        ),
        in_specs=[HBM] * 5,
        out_specs=(VMEM, VMEM, VMEM),
        scratch_shapes=[
            pltpu.VMEM((length, columns), f32),
            pltpu.VMEM((8, length), f32),
            pltpu.SMEM(train_counts.shape, i32),
            pltpu.SMEM(pair_count.shape, i32),
            pltpu.VMEM(points.shape, f32),
            pltpu.VMEM(weights.shape, bf16),
            pltpu.VMEM(pair_slot.shape, i32),
            pltpu.SemaphoreType.DMA((5,)),
        ],
        compiler_params=pltpu.CompilerParams(vmem_limit_bytes=VMEM_LIMIT),
        cost_estimate=pl.CostEstimate(flops=40_000_000, bytes_accessed=4_000_000, transcendentals=0),
        name="prepare",
    )(*stay(train_counts, pair_count, points, weights, pair_slot))


def main_kernel(
    train_counts_hbm, received_ref, packed_weights_ref, packed_points_ref, packed_times_ref,
    partial_ref,
    rows_ref, sums_ref, block_slot, slot_row, train_counts_ref, sem,
):
    fetch = pltpu.make_async_copy(train_counts_hbm, train_counts_ref, sem)
    fetch.start()
    slots, test_tile, columns = partial_ref.shape
    senders = received_ref.shape[0] // slots
    own_tiles = train_counts_ref.shape[0] // senders
    depth = packed_points_ref.shape[0]
    row8 = lax.broadcasted_iota(i32, (8, test_tile), 0)
    per_slot = test_tile // BLOCK
    early = sums_ref.shape[0] * 3 // 10 // BLOCK * BLOCK
    sums_ref[:early, :] = jnp.zeros((early, columns), f32)
    together = math.gcd(slots, 16)

    def place(step, offset):
        operands, counts = [], []
        for i in range(together):
            g = step * together + i
            got = received_ref[g * senders]
            for s in range(1, senders):
                got = got + received_ref[g * senders + s]
            counts.append(jnp.max(got[3:4, :]).astype(i32))
            v = SCALE * (jnp.concatenate([got, got], axis=0) - 1.0)
            square = jnp.sum(jnp.where(row8 < 3, v * v, 0.0), axis=0, keepdims=True)
            raw = jnp.where(
                row8 < 3, -2.0 * v, jnp.where(row8 == 3, 1.0, jnp.where(row8 == 4, square, 0.0))
            )
            high, mid, low = split3(raw)
            spare = jnp.zeros((rows_ref.shape[1] - depth, test_tile), f32)
            operands.append(
                jnp.concatenate([high, high, mid, mid, high, low, spare], axis=0).astype(bf16).T
            )
        for i in range(together):
            g = step * together + i
            start = pl.multiple_of(offset * BLOCK, BLOCK)
            rows_ref[pl.ds(start, test_tile), :] = operands[i]
            slot_row[g] = offset
            for b in range(per_slot):
                block_slot[offset + b] = g
            offset = offset + (counts[i] + BLOCK - 1) // BLOCK
        return offset

    blocks = lax.fori_loop(0, slots // together, place, jnp.int32(0))
    fetch.wait()
    first_tile = lax.axis_index("narrow") * own_tiles
    total = lax.fori_loop(
        0, own_tiles, lambda t, a: a + train_counts_ref[first_tile + t], jnp.int32(0)
    )
    for b in range(2 * PART):
        block_slot[blocks + b] = 0
    parts = (blocks + PART - 1) // PART
    parts = jnp.where(parts < 3, 3, jnp.where(parts == 5, 6, parts))
    steps = (parts + PARTS - 1) // PARTS
    shorter = PARTS * steps - parts
    longer = steps - shorter
    col_tiles = (total + COLS - 1) // COLS
    nothing = jnp.zeros((BLOCK, DEPTH), bf16)
    ring = PARTS * PART

    def with_accumulators(*accs):
        square_accs, sum_accs = accs[: ring + 1], accs[ring + 1 :]
        for acc in accs:
            pltpu.matmul_pop(acc)
        late = sums_ref.shape[0] - early
        sums_ref[early:, :] = jnp.zeros((late, columns), f32)

        def push_points(c):
            rows = packed_points_ref[:, pl.ds(pl.multiple_of(c * COLS, COLS), COLS)]
            pltpu.matmul_push_rhs(
                jnp.concatenate([rows, jnp.zeros((DEPTH - depth, COLS), bf16)], axis=0), 0, 0
            )

        def take_points():
            pltpu.matmul_acc_lhs(square_accs[ring], nothing, load_staged_rhs=0)

        def push_weights(c):
            rows = packed_weights_ref[pl.ds(pl.multiple_of(c * COLS, COLS), COLS), :]
            pltpu.matmul_push_rhs(
                jnp.concatenate([rows, jnp.zeros((COLS, DEPTH - columns), bf16)], axis=1), 0, 1
            )

        def take_weights():
            pltpu.matmul_acc_lhs(sum_accs[ring], nothing, load_staged_rhs=0)

        def block_rows(part, b):
            return pl.ds(pl.multiple_of(part * (PART * BLOCK) + b * BLOCK, BLOCK), BLOCK)

        def start_squares(part, b):
            rows = rows_ref[block_rows(part, b), :]
            pltpu.matmul_acc_lhs(
                square_accs[b],
                jnp.concatenate([rows, jnp.zeros((BLOCK, DEPTH - rows.shape[1]), bf16)], axis=1),
            )

        def gather_sums(part, b):
            rows = block_rows(part, b)
            sums_ref[rows, :] = sums_ref[rows, :] + pltpu.matmul_pop(sum_accs[b])[:, :columns]

        def evaluate(c, part, count, after, before):
            col = pl.ds(pl.multiple_of(c * COLS, COLS), COLS)
            for b in range(ring):
                square = pltpu.matmul_pop(square_accs[b])
                start_squares(after, b)
                gather_sums(before, b)
                if b < count * PART:
                    square = jnp.maximum(square, 1e-30)
                    times = packed_times_ref[pl.ds(block_slot[part * PART + b], 1), col]
                    falloff = jnp.maximum(SCALE - square * lax.rsqrt(square), 0.0)
                    second = falloff * falloff
                    kernel = (second * second * (1.25 * SCALE - falloff) * times).astype(bf16)
                    pltpu.matmul_acc_lhs(sum_accs[b], kernel)

        def last_step(c, before, count):
            take_points()
            push_weights(c + 1)
            evaluate(c, parts - count, count, 0, before)
            take_weights()
            push_points(jnp.minimum(c + 2, col_tiles))

        def col_step(c, before):
            def long_step(q, before):
                part = PARTS * q
                evaluate(c, part, PARTS, part + PARTS, before)
                return part

            def short_step(q, before):
                part = PARTS * longer + (PARTS - 1) * q
                evaluate(c, part, PARTS - 1, part + (PARTS - 1), before)
                return part

            before = lax.fori_loop(0, longer - (shorter == 0).astype(i32), long_step, before)
            before = lax.fori_loop(0, shorter - 1, short_step, before)
            pl.when(shorter == 0)(functools.partial(last_step, c, before, PARTS))
            pl.when(shorter > 0)(functools.partial(last_step, c, before, PARTS - 1))
            return parts - jnp.where(shorter == 0, PARTS, PARTS - 1)

        push_points(jnp.int32(0))
        take_points()
        push_points(jnp.int32(1))
        push_weights(jnp.int32(0))
        take_weights()
        for b in range(ring):
            start_squares(jnp.int32(0), b)
        before = lax.fori_loop(0, col_tiles, col_step, jnp.int32(0))
        for b in range(ring):
            gather_sums(before, b)
            pltpu.matmul_pop(square_accs[b])
        take_points()
        pltpu.matmul_pop(square_accs[ring])
        pltpu.matmul_pop(sum_accs[ring])

    pl.run_scoped(
        with_accumulators,
        *[pltpu.ACC(mxu)((BLOCK, DEPTH), f32) for mxu in range(2) for _ in range(ring + 1)],
    )

    def give(step, carry):
        for i in range(together):
            g = step * together + i
            start = pl.multiple_of(slot_row[g] * BLOCK, BLOCK)
            partial_ref[g] = sums_ref[pl.ds(start, test_tile), :].astype(bf16)
        return carry

    lax.fori_loop(0, slots // together, give, 0)


def partials(train_counts, received, packed, slots, columns):
    test_tile = received.shape[2]
    step_rows = PARTS * PART * BLOCK
    height = max(slots * test_tile, 6 * PART * BLOCK) + step_rows
    return pl.pallas_call(
        main_kernel,
        out_shape=jax.ShapeDtypeStruct((slots, test_tile, columns), bf16),
        in_specs=[HBM, VMEM, VMEM, VMEM, VMEM],
        out_specs=VMEM,
        scratch_shapes=[
            pltpu.VMEM((height, 128), bf16),
            pltpu.VMEM((height, columns), f32),
            pltpu.SMEM((height // BLOCK,), i32),
            pltpu.SMEM((slots,), i32),
            pltpu.SMEM(train_counts.shape, i32),
            pltpu.SemaphoreType.DMA(()),
        ],
        compiler_params=pltpu.CompilerParams(vmem_limit_bytes=VMEM_LIMIT),
        cost_estimate=pl.CostEstimate(flops=3_000_000_000, bytes_accessed=4_000_000, transcendentals=8_000_000),
        name="partials",
    )(*stay(train_counts), received, *packed)


def collect_kernel(shift, slot_tile_ref, collected_ref, out_ref, sums_ref):
    sources = collected_ref.shape[0]
    tiles = out_ref.shape[0]
    group = lax.axis_index("wide")
    first = lax.rem(lax.axis_index("narrow") + shift, lax.axis_size("narrow")) * tiles
    sums_ref[...] = jnp.zeros(sums_ref.shape, f32)
    for w in range(sources):
        tile = slot_tile_ref[w, group] - first
        spot = jnp.where(jnp.logical_and(tile >= 0, tile < tiles), tile, tiles)
        sums_ref[spot] = sums_ref[spot] + collected_ref[w].astype(f32)
    for t in range(tiles):
        out_ref[t] = sums_ref[t].astype(out_ref.dtype)


def collect(shift, slot_tile, collected, tiles, dtype):
    return pl.pallas_call(
        functools.partial(collect_kernel, shift),
        out_shape=jax.ShapeDtypeStruct((tiles,) + collected.shape[1:], dtype),
        in_specs=[SMEM, VMEM],
        out_specs=VMEM,
        scratch_shapes=[pltpu.VMEM((tiles + 1,) + collected.shape[1:], f32)],
        compiler_params=pltpu.CompilerParams(vmem_limit_bytes=VMEM_LIMIT),
        cost_estimate=pl.CostEstimate(flops=1_000_000, bytes_accessed=700_000, transcendentals=0),
        name="collect",
    )(slot_tile, collected)


def body(
    train_points, train_weights, train_counts, test_points, prior, test_counts, pair_count, pair_slot, slot_tile
):
    narrow_size = lax.axis_size("narrow")
    own_tests = test_points.shape[0]
    slots = slot_tile.shape[0]
    columns = train_weights.shape[2]
    offered = offer(slot_tile, test_counts, jnp.transpose(test_points, (1, 0, 2)), slots * narrow_size)
    received = lax.all_to_all(offered, ("wide", "narrow"), 0, 0, tiled=True)
    packed = prepare(
        train_counts, pair_count, jnp.transpose(train_points, (1, 0, 2)), train_weights, pair_slot, slots
    )
    partial_value = partials(train_counts, received, packed, slots, columns)
    collected = lax.all_to_all(partial_value, "wide", 0, 0, tiled=True)
    arrived = []
    for k in range(1, narrow_size):
        sent = collect(k, slot_tile, collected, own_tests, bf16)
        arrived.append(
            lax.ppermute(sent, "narrow", [(i, (i + k) % narrow_size) for i in range(narrow_size)])
        )
    owned = collect(0, slot_tile, collected, own_tests, f32)
    for part in arrived:
        owned = owned + part.astype(f32)
    test_live = jnp.arange(prior.shape[1], dtype=i32)[None, :] < test_counts[:, None]
    update = jnp.where(test_live[:, :, None], owned, 0.0)
    return (prior.astype(f32) + update).astype(bf16)


def solution(mesh):
    return jax.shard_map(
        body,
        mesh=mesh,
        in_specs=(
            P("wide", None, None),
            P(("wide", "narrow"), None, None),
            P("wide"),
            P(("wide", "narrow"), None, None),
            P(("wide", "narrow"), None, None),
            P(("wide", "narrow")),
            P("wide"),
            P("wide", None),
            P(),
        ),
        out_specs=P(("wide", "narrow"), None, None),
        check_vma=False,
    )
```

```python
import functools
import math

import jax
import jax.numpy as jnp
from jax import lax
from jax.experimental import pallas as pl
from jax.experimental.pallas import tpu as pltpu
from jax.sharding import PartitionSpec as P

f32, bf16, i32 = jnp.float32, jnp.bfloat16, jnp.int32
COLS = 256
BLOCK = 16
PART = 8
PARTS = 4
DEPTH = 256
SCALE = 4.0**0.2
VMEM_LIMIT = 32 * 1024 * 1024
VMEM = pl.BlockSpec(memory_space=pltpu.VMEM)
SMEM = pl.BlockSpec(memory_space=pltpu.SMEM)
HBM = pl.BlockSpec(memory_space=pltpu.HBM)


def split3(x):
    high = x.astype(bf16).astype(f32)
    rest = x - high
    mid = rest.astype(bf16).astype(f32)
    low = (rest - mid).astype(bf16).astype(f32)
    return high, mid, low


def stay(*arrays):
    return [pltpu.with_memory_space_constraint(array, pltpu.HBM) for array in arrays]


def offer_kernel(slot_tile_hbm, test_counts_hbm, test_points_hbm, offer_ref, slot_tile, test_counts, points, sems):
    axes, own_tests, test_tile = points.shape
    senders = offer_ref.shape[0]
    wide_size = slot_tile.shape[0]
    copies = [
        pltpu.make_async_copy(source, target, sems.at[i])
        for i, (source, target) in enumerate(
            ((slot_tile_hbm, slot_tile), (test_counts_hbm, test_counts), (test_points_hbm, points))
        )
    ]
    for copy in copies:
        copy.start()
    first = lax.axis_index("narrow") * own_tests
    group = lax.axis_index("wide")
    copies[1].wait()
    copies[2].wait()
    payloads = [
        jnp.concatenate(
            [
                *(points[axis, t : t + 1, :] for axis in range(axes)),
                jnp.full((1, test_tile), test_counts[t].astype(f32), f32),
            ],
            axis=0,
        )
        for t in range(own_tests)
    ]
    narrow_size = senders // wide_size
    copies[0].wait()

    def step(w, carry):
        wanted = slot_tile[w, group] - first
        chosen = jnp.zeros((axes + 1, test_tile), f32)
        for t in range(own_tests):
            chosen = jnp.where(wanted == t, payloads[t], chosen)
        for n in range(narrow_size):
            offer_ref[w * narrow_size + n] = chosen
        return carry

    lax.fori_loop(0, wide_size, step, 0, unroll=16)


def offer(slot_tile, test_counts, test_points, senders):
    axes, own_tests, test_tile = test_points.shape
    return pl.pallas_call(
        offer_kernel,
        out_shape=jax.ShapeDtypeStruct((senders, axes + 1, test_tile), f32),
        in_specs=[HBM, HBM, HBM],
        out_specs=VMEM,
        scratch_shapes=[
            pltpu.SMEM(slot_tile.shape, i32),
            pltpu.SMEM(test_counts.shape, i32),
            pltpu.VMEM(test_points.shape, f32),
            pltpu.SemaphoreType.DMA((3,)),
        ],
        compiler_params=pltpu.CompilerParams(vmem_limit_bytes=VMEM_LIMIT),
        cost_estimate=pl.CostEstimate(flops=100_000, bytes_accessed=100_000, transcendentals=0),
        name="offer",
    )(*stay(slot_tile, test_counts, test_points))


def prepare_kernel(
    train_counts_hbm, pair_count_hbm, points_hbm, weights_hbm, pair_slot_hbm,
    packed_weights_ref, packed_points_ref, packed_times_ref,
    wide_weights, raw_points, train_counts_ref, pair_count_ref, points_ref, weights_ref, pair_slot_ref, sems,
):
    own_tiles, tile, columns = weights_ref.shape
    copies = [
        pltpu.make_async_copy(source, target, sems.at[i])
        for i, (source, target) in enumerate(
            (
                (train_counts_hbm, train_counts_ref),
                (pair_count_hbm, pair_count_ref),
                (points_hbm, points_ref),
                (weights_hbm, weights_ref),
                (pair_slot_hbm, pair_slot_ref),
            )
        )
    ]
    for copy in copies:
        copy.start()
    for copy in copies:
        copy.wait()
    slots = packed_times_ref.shape[0]
    list_length = pair_slot_ref.shape[1]
    first_tile = lax.axis_index("narrow") * own_tiles
    window = tile + 128
    positions = lax.broadcasted_iota(i32, (1, list_length), 1)
    named = pair_slot_ref[...]
    one_hot = (
        lax.broadcasted_iota(i32, (slots, list_length), 0) == jnp.broadcast_to(named, (slots, list_length))
    ).astype(f32)
    row8 = lax.broadcasted_iota(i32, (8, tile), 0)
    lane = lax.broadcasted_iota(i32, (8, window), 1)
    lane_slots = lax.broadcasted_iota(i32, (slots, window), 1)

    def skip(t, total):
        return total + pair_count_ref[t]

    first_pair = lax.fori_loop(0, first_tile, skip, jnp.int32(0))

    def step(t, carry):
        offset, pair = carry
        u = [
            SCALE * (points_ref[axis, pl.ds(first_tile + t, 1), :] - 1.0)
            for axis in range(points_ref.shape[0])
        ]
        square = u[0] * u[0] + u[1] * u[1] + u[2] * u[2]
        raw = jnp.where(row8 == 4, 1.0, 0.0)
        for row, value in enumerate((*u, square)):
            raw = jnp.where(row8 == row, value, raw)
        pair_end = pair + pair_count_ref[first_tile + t]
        inside = jnp.logical_and(positions >= pair, positions < pair_end)
        times = jnp.sum(jnp.where(inside, one_hot, 0.0), axis=1, keepdims=True)
        shift = lax.rem(offset, 128)
        base = pl.multiple_of(offset - shift, 128)
        rolled = pltpu.roll(
            jnp.concatenate([raw, jnp.zeros((8, 128), f32)], axis=1), shift, 1
        )
        spot = pl.ds(base, window)
        raw_points[:, spot] = jnp.where(lane >= shift, rolled, raw_points[:, spot])
        packed_times_ref[:, spot] = jnp.where(
            lane_slots >= shift, times, packed_times_ref[:, spot]
        )
        wide_weights[pl.ds(offset, tile), :] = weights_ref[t].astype(f32)
        return offset + train_counts_ref[first_tile + t], pair_end

    total, _ = lax.fori_loop(0, own_tiles, step, (jnp.int32(0), first_pair))
    shift = lax.rem(total, 128)
    base = pl.multiple_of(total - shift, 128)
    tail = COLS + 128
    spot = pl.ds(base, tail)
    raw_points[:, spot] = jnp.where(
        lax.broadcasted_iota(i32, (8, tail), 1) >= shift, 0.0, raw_points[:, spot]
    )
    packed_times_ref[:, spot] = jnp.where(
        lax.broadcasted_iota(i32, (slots, tail), 1) >= shift, 0.0, packed_times_ref[:, spot]
    )
    wide_weights[pl.ds(total, COLS), :] = jnp.zeros((COLS, columns), f32)

    def finish(c, carry):
        start = pl.multiple_of(c * COLS, COLS)
        high, mid, low = split3(raw_points[:, pl.ds(start, COLS)])
        packed_points_ref[:, pl.ds(start, COLS)] = jnp.concatenate(
            [high, mid, high, mid, low, high], axis=0
        ).astype(bf16)
        packed_weights_ref[pl.ds(start, COLS), :] = wide_weights[pl.ds(start, COLS), :].astype(bf16)
        return carry

    lax.fori_loop(0, (total + COLS - 1) // COLS, finish, 0)


def prepare(train_counts, pair_count, points, weights, pair_slot, slots):
    own_tiles, tile, columns = weights.shape
    length = own_tiles * tile + COLS + 128
    return pl.pallas_call(
        prepare_kernel,
        out_shape=(
            jax.ShapeDtypeStruct((length, columns), bf16),
            jax.ShapeDtypeStruct((48, length), bf16),
            jax.ShapeDtypeStruct((slots, length), f32),
        ),
        in_specs=[HBM] * 5,
        out_specs=(VMEM, VMEM, VMEM),
        scratch_shapes=[
            pltpu.VMEM((length, columns), f32),
            pltpu.VMEM((8, length), f32),
            pltpu.SMEM(train_counts.shape, i32),
            pltpu.SMEM(pair_count.shape, i32),
            pltpu.VMEM(points.shape, f32),
            pltpu.VMEM(weights.shape, bf16),
            pltpu.VMEM(pair_slot.shape, i32),
            pltpu.SemaphoreType.DMA((5,)),
        ],
        compiler_params=pltpu.CompilerParams(vmem_limit_bytes=VMEM_LIMIT),
        cost_estimate=pl.CostEstimate(flops=40_000_000, bytes_accessed=4_000_000, transcendentals=0),
        name="prepare",
    )(*stay(train_counts, pair_count, points, weights, pair_slot))


def main_kernel(
    train_counts_hbm, received_ref, packed_weights_ref, packed_points_ref, packed_times_ref,
    partial_ref,
    rows_ref, sums_ref, block_slot, slot_row, train_counts_ref, sem,
):
    fetch = pltpu.make_async_copy(train_counts_hbm, train_counts_ref, sem)
    fetch.start()
    slots, test_tile, columns = partial_ref.shape
    senders = received_ref.shape[0] // slots
    own_tiles = train_counts_ref.shape[0] // senders
    depth = packed_points_ref.shape[0]
    row8 = lax.broadcasted_iota(i32, (8, test_tile), 0)
    per_slot = test_tile // BLOCK
    sums_ref[...] = jnp.zeros(sums_ref.shape, f32)
    together = math.gcd(slots, 16)

    def place(step, offset):
        operands, counts = [], []
        for i in range(together):
            g = step * together + i
            got = received_ref[g * senders]
            for s in range(1, senders):
                got = got + received_ref[g * senders + s]
            counts.append(got[3, 0].astype(i32))
            v = SCALE * (jnp.concatenate([got, got], axis=0) - 1.0)
            square = v[0:1] * v[0:1] + v[1:2] * v[1:2] + v[2:3] * v[2:3]
            raw = jnp.where(
                row8 < 3, -2.0 * v, jnp.where(row8 == 3, 1.0, jnp.where(row8 == 4, square, 0.0))
            )
            high, mid, low = split3(raw)
            operand = jnp.concatenate([high, high, mid, mid, high, low], axis=0).T
            lanes = jnp.zeros((test_tile, rows_ref.shape[1] - depth), f32)
            operands.append(jnp.concatenate([operand, lanes], axis=1).astype(bf16))
        for i in range(together):
            g = step * together + i
            start = pl.multiple_of(offset * BLOCK, BLOCK)
            rows_ref[pl.ds(start, test_tile), :] = operands[i]
            slot_row[g] = offset
            for b in range(per_slot):
                block_slot[offset + b] = g
            offset = offset + (counts[i] + BLOCK - 1) // BLOCK
        return offset

    blocks = lax.fori_loop(0, slots // together, place, jnp.int32(0))
    fetch.wait()
    first_tile = lax.axis_index("narrow") * own_tiles
    total = lax.fori_loop(
        0, own_tiles, lambda t, a: a + train_counts_ref[first_tile + t], jnp.int32(0)
    )
    for b in range(2 * PART):
        block_slot[blocks + b] = 0
    parts = (blocks + PART - 1) // PART
    parts = jnp.where(parts < 3, 3, jnp.where(parts == 5, 6, parts))
    steps = (parts + PARTS - 1) // PARTS
    shorter = PARTS * steps - parts
    longer = steps - shorter
    col_tiles = (total + COLS - 1) // COLS
    nothing = jnp.zeros((BLOCK, DEPTH), bf16)
    ring = PARTS * PART

    def with_accumulators(*accs):
        square_accs, sum_accs = accs[: ring + 1], accs[ring + 1 :]
        for acc in accs:
            pltpu.matmul_pop(acc)

        def push_points(c):
            rows = packed_points_ref[:, pl.ds(pl.multiple_of(c * COLS, COLS), COLS)]
            pltpu.matmul_push_rhs(
                jnp.concatenate([rows, jnp.zeros((DEPTH - depth, COLS), bf16)], axis=0), 0, 0
            )

        def take_points():
            pltpu.matmul_acc_lhs(square_accs[ring], nothing, load_staged_rhs=0)

        def push_weights(c):
            rows = packed_weights_ref[pl.ds(pl.multiple_of(c * COLS, COLS), COLS), :]
            pltpu.matmul_push_rhs(
                jnp.concatenate([rows, jnp.zeros((COLS, DEPTH - columns), bf16)], axis=1), 0, 1
            )

        def take_weights():
            pltpu.matmul_acc_lhs(sum_accs[ring], nothing, load_staged_rhs=0)

        def block_rows(part, b):
            return pl.ds(pl.multiple_of(part * (PART * BLOCK) + b * BLOCK, BLOCK), BLOCK)

        def start_squares(part, b):
            rows = rows_ref[block_rows(part, b), :]
            pltpu.matmul_acc_lhs(
                square_accs[b],
                jnp.concatenate([rows, jnp.zeros((BLOCK, DEPTH - rows.shape[1]), bf16)], axis=1),
            )

        def gather_sums(part, b):
            rows = block_rows(part, b)
            sums_ref[rows, :] = sums_ref[rows, :] + pltpu.matmul_pop(sum_accs[b])[:, :columns]

        def evaluate(c, part, count, after, before):
            col = pl.ds(pl.multiple_of(c * COLS, COLS), COLS)
            for b in range(ring):
                square = pltpu.matmul_pop(square_accs[b])
                start_squares(after, b)
                gather_sums(before, b)
                if b < count * PART:
                    square = jnp.maximum(square, 1e-30)
                    times = packed_times_ref[pl.ds(block_slot[part * PART + b], 1), col]
                    falloff = jnp.maximum(SCALE - square * lax.rsqrt(square), 0.0)
                    second = falloff * falloff
                    kernel = (second * second * (1.25 * SCALE - falloff) * times).astype(bf16)
                    pltpu.matmul_acc_lhs(sum_accs[b], kernel)

        def last_step(c, before, count):
            take_points()
            push_weights(c + 1)
            evaluate(c, parts - count, count, 0, before)
            take_weights()
            push_points(jnp.minimum(c + 2, col_tiles))

        def col_step(c, before):
            def long_step(q, before):
                part = PARTS * q
                evaluate(c, part, PARTS, part + PARTS, before)
                return part

            def short_step(q, before):
                part = PARTS * longer + (PARTS - 1) * q
                evaluate(c, part, PARTS - 1, part + (PARTS - 1), before)
                return part

            before = lax.fori_loop(0, longer - (shorter == 0).astype(i32), long_step, before)
            before = lax.fori_loop(0, shorter - 1, short_step, before)
            pl.when(shorter == 0)(functools.partial(last_step, c, before, PARTS))
            pl.when(shorter > 0)(functools.partial(last_step, c, before, PARTS - 1))
            return parts - jnp.where(shorter == 0, PARTS, PARTS - 1)

        push_points(jnp.int32(0))
        take_points()
        push_points(jnp.int32(1))
        push_weights(jnp.int32(0))
        take_weights()
        for b in range(ring):
            start_squares(jnp.int32(0), b)
        before = lax.fori_loop(0, col_tiles, col_step, jnp.int32(0))
        for b in range(ring):
            gather_sums(before, b)
            pltpu.matmul_pop(square_accs[b])
        take_points()
        pltpu.matmul_pop(square_accs[ring])
        pltpu.matmul_pop(sum_accs[ring])

    pl.run_scoped(
        with_accumulators,
        *[pltpu.ACC(mxu)((BLOCK, DEPTH), f32) for mxu in range(2) for _ in range(ring + 1)],
    )

    def give(step, carry):
        for i in range(together):
            g = step * together + i
            start = pl.multiple_of(slot_row[g] * BLOCK, BLOCK)
            partial_ref[g] = sums_ref[pl.ds(start, test_tile), :].astype(bf16)
        return carry

    lax.fori_loop(0, slots // together, give, 0)


def partials(train_counts, received, packed, slots, columns):
    test_tile = received.shape[2]
    step_rows = PARTS * PART * BLOCK
    height = max(slots * test_tile, 6 * PART * BLOCK) + step_rows
    return pl.pallas_call(
        main_kernel,
        out_shape=jax.ShapeDtypeStruct((slots, test_tile, columns), bf16),
        in_specs=[HBM, VMEM, VMEM, VMEM, VMEM],
        out_specs=VMEM,
        scratch_shapes=[
            pltpu.VMEM((height, 128), bf16),
            pltpu.VMEM((height, columns), f32),
            pltpu.SMEM((height // BLOCK,), i32),
            pltpu.SMEM((slots,), i32),
            pltpu.SMEM(train_counts.shape, i32),
            pltpu.SemaphoreType.DMA(()),
        ],
        compiler_params=pltpu.CompilerParams(vmem_limit_bytes=VMEM_LIMIT),
        cost_estimate=pl.CostEstimate(flops=3_000_000_000, bytes_accessed=4_000_000, transcendentals=8_000_000),
        name="partials",
    )(*stay(train_counts), received, *packed)


def collect_kernel(shift, slot_tile_ref, collected_ref, out_ref, sums_ref):
    sources = collected_ref.shape[0]
    tiles = out_ref.shape[0]
    group = lax.axis_index("wide")
    first = lax.rem(lax.axis_index("narrow") + shift, lax.axis_size("narrow")) * tiles
    sums_ref[...] = jnp.zeros(sums_ref.shape, f32)
    for w in range(sources):
        tile = slot_tile_ref[w, group] - first
        spot = jnp.where(jnp.logical_and(tile >= 0, tile < tiles), tile, tiles)
        sums_ref[spot] = sums_ref[spot] + collected_ref[w].astype(f32)
    for t in range(tiles):
        out_ref[t] = sums_ref[t].astype(out_ref.dtype)


def collect(shift, slot_tile, collected, tiles, dtype):
    return pl.pallas_call(
        functools.partial(collect_kernel, shift),
        out_shape=jax.ShapeDtypeStruct((tiles,) + collected.shape[1:], dtype),
        in_specs=[SMEM, VMEM],
        out_specs=VMEM,
        scratch_shapes=[pltpu.VMEM((tiles + 1,) + collected.shape[1:], f32)],
        compiler_params=pltpu.CompilerParams(vmem_limit_bytes=VMEM_LIMIT),
        cost_estimate=pl.CostEstimate(flops=1_000_000, bytes_accessed=700_000, transcendentals=0),
        name="collect",
    )(slot_tile, collected)


def body(
    train_points, train_weights, train_counts, test_points, prior, test_counts, pair_count, pair_slot, slot_tile
):
    narrow_size = lax.axis_size("narrow")
    own_tests = test_points.shape[0]
    slots = slot_tile.shape[0]
    columns = train_weights.shape[2]
    offered = offer(slot_tile, test_counts, jnp.transpose(test_points, (1, 0, 2)), slots * narrow_size)
    received = lax.all_to_all(offered, ("wide", "narrow"), 0, 0, tiled=True)
    packed = prepare(
        train_counts, pair_count, jnp.transpose(train_points, (1, 0, 2)), train_weights, pair_slot, slots
    )
    partial_value = partials(train_counts, received, packed, slots, columns)
    collected = lax.all_to_all(partial_value, "wide", 0, 0, tiled=True)
    arrived = []
    for k in range(1, narrow_size):
        sent = collect(k, slot_tile, collected, own_tests, bf16)
        arrived.append(
            lax.ppermute(sent, "narrow", [(i, (i + k) % narrow_size) for i in range(narrow_size)])
        )
    owned = collect(0, slot_tile, collected, own_tests, f32)
    for part in arrived:
        owned = owned + part.astype(f32)
    test_live = jnp.arange(prior.shape[1], dtype=i32)[None, :] < test_counts[:, None]
    update = jnp.where(test_live[:, :, None], owned, 0.0)
    return (prior.astype(f32) + update).astype(bf16)


def solution(mesh):
    return jax.shard_map(
        body,
        mesh=mesh,
        in_specs=(
            P("wide", None, None),
            P(("wide", "narrow"), None, None),
            P("wide"),
            P(("wide", "narrow"), None, None),
            P(("wide", "narrow"), None, None),
            P(("wide", "narrow")),
            P("wide"),
            P("wide", None),
            P(),
        ),
        out_specs=P(("wide", "narrow"), None, None),
        check_vma=False,
    )
```
